32 devices in a mesh: row: 8 (over y, x, core), col: 4 (over z).
Axes of the slice: x: 2, y: 2, z: 4, core: 2. Of those that a mesh axis runs over, the one named last changes fastest.
Arguments:
- features: bfloat16 [8192, 256], P(('row', 'col')), may hold values from -6 to 6
- adjacency: bfloat16 [32, 96, 128, 128], P(('row', 'col')), may hold values from -0.09375 to 0.09375
- tile_row: int32 [32, 96], P(('row', 'col')), may hold values from 0 to 7, as said below
- tile_column: int32 [32, 96], P(('row', 'col')), may hold values from 0 to 15, as said below
- tile_count: int32 [32], P(('row', 'col')), may hold values from 1 to 96, as said below
- weight_in: bfloat16 [256, 1024], replicated, may hold values from -0.375 to 0.375
- bias_in: float32 [1024], replicated, may hold values from -3 to 3
- weight_out: bfloat16 [1024, 256], replicated, may hold values from -0.25 to 0.25
- bias_out: float32 [256], replicated, may hold values from -3 to 3
Outputs:
- updated: bfloat16 [8192, 256], P(('row', 'col'))
The draws below stay inside these ranges and needn't reach their ends.
Inputs may be any that keep to these rules, and one draw needn't show every extreme that they name: `tile_row`: for every device and slot s < tile_count, the block row i and block column j of step one satisfy i >= j, and no device names one pair twice. Slots at or beyond tile_count hold coordinates in range that are not part of A. Every device of the highest index along row holds exactly 96 tiles. `tile_column`: see tile_row. `tile_count`: every device of the highest index along row has the most.
All inputs are finite; a program needn't handle non-finite values.
Results may differ from the reference program's by a relative error of at most 0.0056.
Values may be sent and summed in bfloat16 or wider, within the bound.
A program may use at most 128 MiB of HBM per device.

```python
import jax
import jax.numpy as jnp
from jax import lax

TILE = 128
F = 256
HID = 1024
BLK_DEV = 2
BLOCKS = 64
VERTICES = 8192
ROW_BLOCKS = 8
COL_BLOCKS = 16
CAP = 96
DEVICES = 32


def tile_layout(key):
    base = jax.random.fold_in(key, 11)
    col_count = ROW_BLOCKS // BLK_DEV
    device_count = BLOCKS // BLK_DEV
    row_count = device_count // col_count
    pairs = ROW_BLOCKS * COL_BLOCKS

    def one_device(device):
        row_index = device // col_count
        col_index = device % col_count
        candidate = jnp.arange(pairs, dtype=jnp.int32)
        local_rows = candidate // COL_BLOCKS
        local_cols = candidate % COL_BLOCKS
        block_i = row_index * ROW_BLOCKS + local_rows
        block_j = (local_cols // BLK_DEV * col_count + col_index) * BLK_DEV + local_cols % BLK_DEV
        valid = block_i >= block_j
        priority = jax.random.permutation(jax.random.fold_in(base, device), pairs).astype(jnp.int32)
        score = jnp.where(valid, priority, priority + pairs)
        picked = jnp.argsort(score)[:CAP]
        filled = jnp.minimum(jnp.sum(valid.astype(jnp.int32)), CAP).astype(jnp.int32)
        keep = jnp.arange(CAP, dtype=jnp.int32) < filled
        rows_out = jnp.where(keep, local_rows[picked], 0).astype(jnp.int32)
        cols_out = jnp.where(keep, local_cols[picked], 0).astype(jnp.int32)
        lowest = jnp.maximum(filled // 2, 1).astype(jnp.int32)
        drawn = jax.random.randint(jax.random.fold_in(base, device + 100003), (), lowest, filled + 1).astype(jnp.int32)
        count = jnp.where(row_index == row_count - 1, filled, drawn).astype(jnp.int32)
        return (rows_out, cols_out, count)
    return jax.vmap(one_device)(jnp.arange(device_count, dtype=jnp.int32))


def draw_tile_row(key, part):
    return tile_layout(key)[0]


def draw_tile_column(key, part):
    return tile_layout(key)[1]


def draw_tile_count(key, part):
    return tile_layout(key)[2]


def levels(rng, shape, split, low, top_value):
    def one(position, shards_of):
        heights = jax.random.uniform(jax.random.fold_in(jax.random.fold_in(rng, 6), position), (shards_of,), jnp.float32, low / len(split), top_value / len(split))
        return jnp.repeat(jnp.exp(heights), shape[position] // shards_of).reshape((-1,) + (1,) * (len(shape) - position - 1))

    level = one(*split[0])
    for cut in split[1:]:
        level = level * one(*cut)
    return level


def noise(own_key, extent, scale, reach, pieces=(), held_as=jnp.bfloat16):
    values = scale * jax.random.normal(own_key, extent, jnp.float32)
    if pieces:
        values = values * levels(own_key, extent, pieces, -0.22, 0.18)
    return jnp.clip(values, -reach, reach).astype(held_as)


def setup_inputs(seed: int = 0) -> dict:
    splits = jax.random.split(jax.random.key(seed), 10)
    features = noise(splits[0], (VERTICES, F), 1.0, 6.0, ((0, 32),))
    adjacency = noise(splits[1], (DEVICES, CAP, TILE, TILE), (TILE * BLOCKS // 2) ** -0.5, 0.09375, ((0, 32),))
    tile_row = draw_tile_row(jax.random.fold_in(splits[9], 71), 0)
    tile_column = draw_tile_column(jax.random.fold_in(splits[9], 71), 0)
    tile_count = draw_tile_count(jax.random.fold_in(splits[9], 71), 0)
    weight_in = noise(splits[5], (F, HID), F ** -0.5, 0.375)
    bias_in = noise(splits[6], (HID,), 0.5, 3.0, (), jnp.float32)
    weight_out = noise(splits[7], (HID, F), (HID // 2) ** -0.5, 0.25)
    bias_out = noise(splits[8], (F,), 0.5, 3.0, (), jnp.float32)
    return {"features": features, "adjacency": adjacency, "tile_row": tile_row, "tile_column": tile_column, "tile_count": tile_count, "weight_in": weight_in, "bias_in": bias_in, "weight_out": weight_out, "bias_out": bias_out}


def reference(features, adjacency, tile_row, tile_column, tile_count, weight_in, bias_in, weight_out, bias_out):
    col_count = ROW_BLOCKS // BLK_DEV
    device_count = BLOCKS // BLK_DEV
    vertex_blocks = features.reshape(BLOCKS, TILE, F).astype(jnp.float32)
    slot_index = jnp.arange(CAP, dtype=jnp.int32)

    def per_device(total, device):
        row_index = device // col_count
        col_index = device % col_count
        local_rows = tile_row[device].astype(jnp.int32)
        local_cols = tile_column[device].astype(jnp.int32)
        block_i = (row_index * ROW_BLOCKS + local_rows).astype(jnp.int32)
        block_j = (((local_cols // BLK_DEV) * col_count + col_index) * BLK_DEV + local_cols % BLK_DEV).astype(jnp.int32)
        live = (slot_index < tile_count[device]).astype(jnp.float32)
        tile_values = adjacency[device].astype(jnp.float32)
        to_rows = jnp.einsum("kab,kbf->kaf", tile_values, vertex_blocks[block_j], precision=lax.Precision.HIGHEST)
        to_cols = jnp.einsum("kab,kaf->kbf", tile_values, vertex_blocks[block_i], precision=lax.Precision.HIGHEST)
        to_rows = to_rows * live[:, None, None]
        to_cols = to_cols * live[:, None, None]
        total = total.at[block_i].add(to_rows).at[block_j].add(to_cols)
        return total, None

    start = jnp.zeros((BLOCKS, TILE, F), jnp.float32)
    total, _ = lax.scan(per_device, start, jnp.arange(device_count, dtype=jnp.int32))
    combined = (features.astype(jnp.float32) + total.reshape(VERTICES, F)).astype(jnp.bfloat16)
    hidden = jax.nn.relu(jnp.dot(combined, weight_in, preferred_element_type=jnp.float32) + bias_in).astype(jnp.bfloat16)
    updated = jnp.dot(hidden, weight_out, preferred_element_type=jnp.float32) + bias_out
    return updated.astype(jnp.bfloat16)
```

```python
import functools

import jax
import jax.numpy as jnp
from jax import lax
from jax.experimental import pallas as pl
from jax.experimental.pallas import tpu as pltpu
from jax.sharding import PartitionSpec as P

TILE = 128
CORES = 2
CHUNKS = 2
MESH = pl.DeviceIdType.MESH


def both(*conditions):
    result = conditions[0]
    for condition in conditions[1:]:
        result = jnp.logical_and(result, condition)
    return result


def kernel(
    n_row,
    n_col,
    x_ref,
    adjacency_ref,
    tile_row_ref,
    tile_column_ref,
    count_ref,
    weight_in_ref,
    bias_in_ref,
    weight_out_ref,
    bias_out_ref,
    out_ref,
    adj,
    dense,
    keys,
    slots_v,
    slots,
    w_in,
    w_out,
    xcol,
    xrow,
    acc_r,
    acc_c,
    row_send,
    row_up,
    row_down,
    sib_send,
    sib_recv,
    col_send,
    col_recv,
    combined,
    local_sem,
    gather_up_sem,
    gather_down_sem,
    gather_recv_sem,
    plane_send_sem,
    plane_recv_sem,
    sibling_send_sem,
    up_send_sem,
    up_recv_sem,
    down_send_sem,
    down_recv_sem,
    pair_send_sem,
    pair_recv_sem,
    col_send_sem,
    col_recv_sem,
):
    chunks, _, fw, rows = xrow.shape
    blocks = rows // TILE
    cap = adjacency_ref.shape[1]
    row_blocks = n_col * blocks
    col_blocks = n_row * blocks
    places = row_blocks * col_blocks
    chips = n_row // CORES
    r = lax.axis_index("row")
    c = lax.axis_index("col")
    k = r // CORES
    q = r % CORES
    other = 1 - q
    sibling = (k * CORES + other, c)
    above = (r, c + 1)
    below = (r, c - 1)
    pending = []

    def send(condition, make):
        @pl.when(condition)
        def _():
            make().start()

        pending.append((condition, make))

    def remote(src, dst, send_sem, recv_sem, device):
        return pltpu.make_async_remote_copy(
            src_ref=src,
            dst_ref=dst,
            send_sem=send_sem,
            recv_sem=recv_sem,
            device_id=device,
            device_id_type=MESH,
        )

    def arrived(dst, sem):
        pltpu.make_async_copy(dst, dst, sem).wait()

    barrier = pltpu.get_barrier_semaphore()
    pl.semaphore_signal(barrier, inc=1, device_id=sibling, device_id_type=MESH)
    for kk in range(chips):

        @pl.when(k != kk)
        def _():
            pl.semaphore_signal(
                barrier, inc=1, device_id=(kk * CORES + q, c), device_id_type=MESH
            )

    @pl.when(c > 0)
    def _():
        pl.semaphore_signal(barrier, inc=1, device_id=below, device_id_type=MESH)

    @pl.when(c < n_col - 1)
    def _():
        pl.semaphore_signal(barrier, inc=1, device_id=above, device_id_type=MESH)

    adj_copy = pltpu.make_async_copy(
        adjacency_ref.at[0], adj.at[pl.ds(0, cap)], local_sem.at[0]
    )
    adj_copy.start()
    in_copy = pltpu.make_async_copy(weight_in_ref, w_in, local_sem.at[1])
    in_copy.start()
    out_copy = pltpu.make_async_copy(weight_out_ref, w_out, local_sem.at[2])
    out_copy.start()

    x = x_ref[...]
    xt = x.T
    for h in range(chunks):
        xcol[h, r] = x[:, h * fw : (h + 1) * fw]
        xrow[h, c] = xt[h * fw : (h + 1) * fw, :]

    has_below = (c + n_col - 1) // n_col
    has_above = (2 * n_col - 2 - c) // n_col
    pl.semaphore_wait(barrier, chips + has_below + has_above)

    def gather_send(h, b, up):
        device = above if up else below
        sem = gather_up_sem if up else gather_down_sem
        return remote(
            xrow.at[h, b], xrow.at[h, b], sem.at[h, b], gather_recv_sem.at[h, b], device
        )

    def gather_own(h):
        send(c < n_col - 1, functools.partial(gather_send, h, c, True))
        send(c > 0, functools.partial(gather_send, h, c, False))

    def sibling_send(h, b):
        return remote(
            xcol.at[h, b],
            xcol.at[h, b],
            sibling_send_sem.at[h, b],
            plane_recv_sem.at[h, b],
            sibling,
        )

    def plane_own(h):
        for kk in range(1, chips):
            send(
                kk > k,
                lambda kk=kk: remote(
                    xcol.at[h, r],
                    xcol.at[h, r],
                    plane_send_sem.at[h, kk],
                    plane_recv_sem.at[h, r],
                    (kk * CORES + q, c),
                ),
            )
        send(q == 0, functools.partial(sibling_send, h, r))

    gather_own(0)
    for h in range(chunks):
        plane_own(h)

    wide = keys.shape[1]
    keys[...] = jnp.full(keys.shape, -1, jnp.int32)
    slot_row = lax.broadcasted_iota(jnp.int32, (1, cap), 1)
    keys[0:1, 0:cap] = jnp.where(
        slot_row < count_ref[0],
        tile_row_ref[...] * col_blocks + tile_column_ref[...],
        -1,
    )
    key_column = jnp.broadcast_to(keys[0:1, :], (TILE, wide)).T[:, 0:1]
    hit = key_column == lax.broadcasted_iota(jnp.int32, (wide, places), 1)
    number = lax.broadcasted_iota(jnp.int32, (wide, places), 0)
    slots_v[...] = cap + jnp.sum(
        jnp.where(hit, number - cap, 0), axis=0, keepdims=True
    )
    slot_copy = pltpu.make_async_copy(slots_v, slots, local_sem.at[3])
    slot_copy.start()
    adj[cap] = jnp.zeros((TILE, TILE), jnp.bfloat16)
    slot_copy.wait()
    adj_copy.wait()

    @pl.loop(0, r + 1)
    def _(owner):
        for i in range(row_blocks):
            for b in range(blocks):
                place = i * col_blocks + owner * blocks + b
                dense[owner, pl.ds(i * TILE, TILE), pl.ds(b * TILE, TILE)] = adj[
                    slots[0, place]
                ]

    def to_rows(h, owner, first=False):
        added = jnp.dot(
            dense[owner], xcol[h, owner], preferred_element_type=jnp.float32
        ).reshape(n_col, rows, fw)
        if first:
            acc_r[h] = added
        else:
            acc_r[h] += added

    def to_cols(h, source, first=False):
        part = pl.ds(pl.multiple_of(source * rows, rows), rows)

        @pl.loop(0, r + 1)
        def _(owner):
            added = jnp.dot(
                xrow[h, source], dense[owner, part, :], preferred_element_type=jnp.float32
            )
            if first:
                acc_c[h, owner] = added
            else:
                acc_c[h, owner] += added

    def gather_step(h, s):
        @pl.when(c - s >= 0)
        def _():
            arrived(xrow.at[h, c - s], gather_recv_sem.at[h, c - s])

        send(both(c - s >= 0, c < n_col - 1), lambda: gather_send(h, c - s, True))

        @pl.when(c + s < n_col)
        def _():
            arrived(xrow.at[h, c + s], gather_recv_sem.at[h, c + s])

        send(both(c + s < n_col, c > 0), lambda: gather_send(h, c + s, False))

        if s == max(n_col - 2, 1) and h + 1 < chunks:
            gather_own(h + 1)

        @pl.when(c - s >= 0)
        def _():
            to_cols(h, c - s)

        @pl.when(c + s < n_col)
        def _():
            to_cols(h, c + s)

    def plane_step(h):
        for kk in reversed(range(chips - 1)):
            owner = kk * CORES + q

            @pl.when(kk < k)
            def _():
                arrived(xcol.at[h, owner], plane_recv_sem.at[h, owner])

            send(kk < k, functools.partial(sibling_send, h, owner))

            @pl.when(kk < k)
            def _():
                to_rows(h, owner)

        @pl.when(q == 1)
        def _():
            arrived(xcol.at[h, r - 1], plane_recv_sem.at[h, r - 1])
            to_rows(h, r - 1)

        for kk in reversed(range(chips - 1)):
            owner = kk * CORES + other

            @pl.when(kk < k)
            def _():
                arrived(xcol.at[h, owner], plane_recv_sem.at[h, owner])
                to_rows(h, owner)

    def reduce_rows(h, t):
        def one(d, ahead, first, last, landing, send_sem, recv_sem, device):
            @pl.when(both(ahead, first))
            def _():
                row_send[h, d] = acc_r[h, d].astype(jnp.bfloat16)

            @pl.when(both(ahead, jnp.logical_not(first)))
            def _():
                arrived(landing.at[h, d], recv_sem.at[h, d])
                row_send[h, d] = (
                    acc_r[h, d] + landing[h, d].astype(jnp.float32)
                ).astype(jnp.bfloat16)

            send(
                ahead,
                lambda: remote(
                    row_send.at[h, d],
                    landing.at[h, d],
                    send_sem.at[h, d],
                    recv_sem.at[h, d],
                    device,
                ),
            )

        up = n_col - 1 - t
        one(up, c < up, c == 0, None, row_up, up_send_sem, up_recv_sem, above)
        one(t, c > t, c == n_col - 1, None, row_down, down_send_sem, down_recv_sem, below)

    def pair_start(h):
        for kk in range(chips):
            condition = jnp.logical_or(kk < k, both(kk == k, q == 1))

            @pl.when(condition)
            def _():
                sib_send[h, kk] = acc_c[h, kk * CORES + other].astype(jnp.bfloat16)

            send(
                condition,
                lambda kk=kk: remote(
                    sib_send.at[h, kk],
                    sib_recv.at[h, kk],
                    pair_send_sem.at[h, kk],
                    pair_recv_sem.at[h, kk],
                    sibling,
                ),
            )

    def reduce_cols(h):
        for kk in range(chips - 1):

            @pl.when(kk < k)
            def _():
                arrived(sib_recv.at[h, kk], pair_recv_sem.at[h, kk])
                col_send[h, kk] = (
                    acc_c[h, kk * CORES + q] + sib_recv[h, kk].astype(jnp.float32)
                ).astype(jnp.bfloat16)

            send(
                kk < k,
                lambda kk=kk: remote(
                    col_send.at[h, kk],
                    col_recv.at[h, k],
                    col_send_sem.at[h, kk],
                    col_recv_sem.at[h, k],
                    (kk * CORES + q, c),
                ),
            )

    def finish(h):
        @pl.when(q == 0)
        def _():
            arrived(sib_recv.at[h, k], pair_recv_sem.at[h, k])
            acc_c[h, r] += sib_recv[h, k].astype(jnp.float32)

        for kk in range(1, chips):

            @pl.when(kk > k)
            def _():
                arrived(col_recv.at[h, kk], col_recv_sem.at[h, kk])
                acc_c[h, r] += col_recv[h, kk].astype(jnp.float32)

        @pl.when(c > 0)
        def _():
            arrived(row_up.at[h, c], up_recv_sem.at[h, c])
            acc_r[h, c] += row_up[h, c].astype(jnp.float32)

        @pl.when(c < n_col - 1)
        def _():
            arrived(row_down.at[h, c], down_recv_sem.at[h, c])
            acc_r[h, c] += row_down[h, c].astype(jnp.float32)

        combined[:, h * fw : (h + 1) * fw] = (
            xcol[h, r].astype(jnp.float32) + acc_r[h, c] + acc_c[h, r].T
        ).astype(jnp.bfloat16)

    for h in range(chunks):
        to_rows(h, r, True)
        to_cols(h, c, True)
    for h in range(chunks):
        gather_step(h, 1)
        if h > 0:
            reduce_cols(h - 1)
        plane_step(h)
        reduce_rows(h, 0)
        for s in range(2, n_col):
            gather_step(h, s)
            if s < n_col - 1:
                reduce_rows(h, s - 1)
        pair_start(h)
        reduce_rows(h, n_col - 2)
    reduce_cols(chunks - 1)
    in_copy.wait()
    out_copy.wait()
    for h in range(chunks):
        finish(h)

    hid = w_in.shape[1]
    part = min(hid, 256)
    total = jnp.zeros(out_ref.shape, jnp.float32) + bias_out_ref[...]
    for j in range(0, hid, part):
        hidden = jnp.dot(
            combined[...], w_in[:, j : j + part], preferred_element_type=jnp.float32
        )
        hidden = jnp.maximum(hidden + bias_in_ref[:, j : j + part], 0.0)
        total += jnp.dot(
            hidden.astype(jnp.bfloat16),
            w_out[j : j + part, :],
            preferred_element_type=jnp.float32,
        )
    out_ref[...] = total.astype(jnp.bfloat16)

    for condition, make in pending:

        @pl.when(condition)
        def _():
            make().wait_send()


def solution(mesh):
    n_row = mesh.shape["row"]
    n_col = mesh.shape["col"]
    chips = n_row // CORES

    def shards(
        features, adjacency, tile_row, tile_column, tile_count, weight_in, bias_in, weight_out, bias_out
    ):
        rows, width = features.shape
        cap = adjacency.shape[1]
        blocks = rows // TILE
        places = n_row * n_col * blocks * blocks
        fw = width // CHUNKS
        bf16, f32 = jnp.bfloat16, jnp.float32
        dma = pltpu.SemaphoreType.DMA
        vmem = pl.BlockSpec(memory_space=pltpu.VMEM)
        anywhere = pl.BlockSpec(memory_space=pl.ANY)
        scratch = [
            pltpu.VMEM((cap + 1, TILE, TILE), bf16),
            pltpu.VMEM((n_row, n_col * rows, rows), bf16),
            pltpu.VMEM((8, -(-cap // TILE) * TILE), jnp.int32),
            pltpu.VMEM((1, places), jnp.int32),
            pltpu.SMEM((1, places), jnp.int32),
            pltpu.VMEM(weight_in.shape, bf16),
            pltpu.VMEM(weight_out.shape, bf16),
            pltpu.VMEM((CHUNKS, n_row, rows, fw), bf16),
            pltpu.VMEM((CHUNKS, n_col, fw, rows), bf16),
            pltpu.VMEM((CHUNKS, n_col, rows, fw), f32),
            pltpu.VMEM((CHUNKS, n_row, fw, rows), f32),
            pltpu.VMEM((CHUNKS, n_col, rows, fw), bf16),
            pltpu.VMEM((CHUNKS, n_col, rows, fw), bf16),
            pltpu.VMEM((CHUNKS, n_col, rows, fw), bf16),
            pltpu.VMEM((CHUNKS, chips, fw, rows), bf16),
            pltpu.VMEM((CHUNKS, chips, fw, rows), bf16),
            pltpu.VMEM((CHUNKS, chips, fw, rows), bf16),
            pltpu.VMEM((CHUNKS, chips, fw, rows), bf16),
            pltpu.VMEM((rows, width), bf16),
            dma((4,)),
            dma((CHUNKS, n_col)),
            dma((CHUNKS, n_col)),
            dma((CHUNKS, n_col)),
            dma((CHUNKS, chips)),
            dma((CHUNKS, n_row)),
            dma((CHUNKS, n_row)),
            dma((CHUNKS, n_col)),
            dma((CHUNKS, n_col)),
            dma((CHUNKS, n_col)),
            dma((CHUNKS, n_col)),
            dma((CHUNKS, chips)),
            dma((CHUNKS, chips)),
            dma((CHUNKS, chips)),
            dma((CHUNKS, chips)),
        ]
        return pl.pallas_call(
            functools.partial(kernel, n_row, n_col),
            out_shape=jax.ShapeDtypeStruct((rows, width), bf16),
            in_specs=[
                vmem,
                anywhere,
                vmem,
                vmem,
                pl.BlockSpec(memory_space=pltpu.SMEM),
                anywhere,
                vmem,
                anywhere,
                vmem,
            ],
            out_specs=vmem,
            scratch_shapes=scratch,
            compiler_params=pltpu.CompilerParams(
                collective_id=0, has_side_effects=True, vmem_limit_bytes=56 * 1024 * 1024
            ),
            name="gin_layer",
        )(
            features,
            adjacency,
            tile_row,
            tile_column,
            tile_count,
            weight_in,
            bias_in.reshape(1, -1),
            weight_out,
            bias_out.reshape(1, -1),
        )

    placed = (
        P(("row", "col"), None),
        P(("row", "col"), None, None, None),
        P(("row", "col"), None),
        P(("row", "col"), None),
        P(("row", "col")),
        P(),
        P(),
        P(),
        P(),
    )
    return jax.shard_map(
        shards, mesh=mesh, in_specs=placed, out_specs=P(("row", "col"), None), check_vma=False
    )
```

```python
import functools

import jax
import jax.numpy as jnp
from jax import lax
from jax.experimental import pallas as pl
from jax.experimental.pallas import tpu as pltpu
from jax.sharding import PartitionSpec as P

TILE = 128
CORES = 2
MESH = pl.DeviceIdType.MESH


def both(*conditions):
    result = conditions[0]
    for condition in conditions[1:]:
        result = jnp.logical_and(result, condition)
    return result


def kernel(
    n_row,
    n_col,
    x_ref,
    adjacency_ref,
    tile_row_ref,
    tile_column_ref,
    count_ref,
    weight_in_ref,
    bias_in_ref,
    weight_out_ref,
    bias_out_ref,
    out_ref,
    adj,
    dense,
    keys,
    slots_v,
    slots,
    w_in,
    w_out,
    xcol,
    xrow,
    acc_r,
    acc_c,
    row_send,
    row_up,
    row_down,
    sib_send,
    sib_recv,
    col_send,
    col_recv,
    local_sem,
    gather_up_sem,
    gather_down_sem,
    gather_recv_sem,
    plane_send_sem,
    plane_recv_sem,
    sibling_send_sem,
    up_send_sem,
    up_recv_sem,
    down_send_sem,
    down_recv_sem,
    pair_send_sem,
    pair_recv_sem,
    col_send_sem,
    col_recv_sem,
):
    _, width, rows = xrow.shape
    blocks = rows // TILE
    cap = adjacency_ref.shape[1]
    row_blocks = n_col * blocks
    col_blocks = n_row * blocks
    places = row_blocks * col_blocks
    chips = n_row // CORES
    wide = CORES * rows
    r = lax.axis_index("row")
    c = lax.axis_index("col")
    k = r // CORES
    q = r % CORES
    other = 1 - q
    sibling = (k * CORES + other, c)
    above = (r, c + 1)
    below = (r, c - 1)
    f32, bf16 = jnp.float32, jnp.bfloat16

    def remote(src, dst, send_sem, recv_sem, device):
        return pltpu.make_async_remote_copy(
            src_ref=src,
            dst_ref=dst,
            send_sem=send_sem,
            recv_sem=recv_sem,
            device_id=device,
            device_id_type=MESH,
        )

    def arrived(dst, sem):
        pltpu.make_async_copy(dst, dst, sem).wait()

    def run(condition, make, start):
        @pl.when(condition)
        def _():
            if start:
                make().start()
            else:
                make().wait_send()

    def gather_copy(b, up):
        sem = gather_up_sem if up else gather_down_sem
        device = above if up else below
        return remote(xrow.at[b], xrow.at[b], sem.at[b], gather_recv_sem.at[b], device)

    def gather_up(b, start):
        run(both(b >= 0, c < n_col - 1), lambda: gather_copy(b, True), start)

    def gather_down(b, start):
        run(both(b < n_col, c > 0), lambda: gather_copy(b, False), start)

    def plane(kk, start):
        run(
            kk > k,
            lambda: remote(
                xcol.at[k, pl.ds(q * rows, rows)],
                xcol.at[k, pl.ds(q * rows, rows)],
                plane_send_sem.at[kk],
                plane_recv_sem.at[r],
                (kk * CORES + q, c),
            ),
            start,
        )

    def to_sibling(kk, start):
        run(
            jnp.logical_or(kk < k, q == 0),
            lambda: remote(
                xcol.at[kk, pl.ds(q * rows, rows)],
                xcol.at[kk, pl.ds(q * rows, rows)],
                sibling_send_sem.at[kk],
                plane_recv_sem.at[kk * CORES + q],
                sibling,
            ),
            start,
        )

    def row_sum(d, up, start):
        run(
            c < d if up else c > d,
            lambda: remote(
                row_send.at[d],
                (row_up if up else row_down).at[d],
                (up_send_sem if up else down_send_sem).at[d],
                (up_recv_sem if up else down_recv_sem).at[d],
                above if up else below,
            ),
            start,
        )

    def pair(kk, start):
        run(
            jnp.logical_or(kk < k, q == 1),
            lambda: remote(
                sib_send.at[kk],
                sib_recv.at[kk],
                pair_send_sem.at[kk],
                pair_recv_sem.at[kk],
                sibling,
            ),
            start,
        )

    def col_sum(kk):
        return remote(
            col_send.at[kk],
            col_recv.at[k],
            col_send_sem.at[kk],
            col_recv_sem.at[k],
            (kk * CORES + q, c),
        )

    barrier = pltpu.get_barrier_semaphore()
    pl.semaphore_signal(barrier, inc=1, device_id=sibling, device_id_type=MESH)
    for kk in range(chips):

        @pl.when(k != kk)
        def _():
            pl.semaphore_signal(
                barrier, inc=1, device_id=(kk * CORES + q, c), device_id_type=MESH
            )

    @pl.when(c > 0)
    def _():
        pl.semaphore_signal(barrier, inc=1, device_id=below, device_id_type=MESH)

    @pl.when(c < n_col - 1)
    def _():
        pl.semaphore_signal(barrier, inc=1, device_id=above, device_id_type=MESH)

    adj_copy = pltpu.make_async_copy(
        adjacency_ref.at[0], adj.at[pl.ds(0, cap)], local_sem.at[0]
    )
    adj_copy.start()
    in_copy = pltpu.make_async_copy(weight_in_ref, w_in, local_sem.at[1])
    in_copy.start()
    out_copy = pltpu.make_async_copy(weight_out_ref, w_out, local_sem.at[2])
    out_copy.start()

    xcol[k, pl.ds(pl.multiple_of(q * rows, rows), rows)] = x_ref[...]
    xrow[c] = x_ref[...].T

    lanes = keys.shape[1]
    keys[...] = jnp.full(keys.shape, -1, jnp.int32)
    slot_row = lax.broadcasted_iota(jnp.int32, (1, cap), 1)
    keys[0:1, 0:cap] = jnp.where(
        slot_row < count_ref[0],
        tile_row_ref[...] * col_blocks + tile_column_ref[...],
        -1,
    )
    key_column = jnp.broadcast_to(keys[0:1, :], (TILE, lanes)).T[:, 0:1]
    hit = key_column == lax.broadcasted_iota(jnp.int32, (lanes, places), 1)
    number = lax.broadcasted_iota(jnp.int32, (lanes, places), 0)
    slots_v[...] = cap + jnp.sum(
        jnp.where(hit, number - cap, 0), axis=0, keepdims=True
    )
    slot_copy = pltpu.make_async_copy(slots_v, slots, local_sem.at[3])
    slot_copy.start()
    adj[cap] = jnp.zeros((TILE, TILE), bf16)

    has_below = (c + n_col - 1) // n_col
    has_above = (2 * n_col - 2 - c) // n_col
    pl.semaphore_wait(barrier, chips + has_below + has_above)

    gather_up(c, True)
    gather_down(c, True)
    to_sibling(k, True)
    for kk in range(1, chips):
        plane(kk, True)

    @pl.when(q == 0)
    def _():
        xcol[k, pl.ds(rows, rows)] = jnp.zeros((rows, width), bf16)

    acc_r[...] = jnp.zeros(acc_r.shape, f32)
    acc_c[...] = jnp.zeros(acc_c.shape, f32)
    slot_copy.wait()
    adj_copy.wait()

    @pl.loop(0, chips)
    def _(kk):
        for i in range(row_blocks):
            for b in range(CORES * blocks):
                place = i * col_blocks + kk * (CORES * blocks) + b
                dense[kk, pl.ds(i * TILE, TILE), pl.ds(b * TILE, TILE)] = adj[
                    slots[0, place]
                ]

    def to_cols(source):
        part = pl.ds(pl.multiple_of(source * rows, rows), rows)
        for kk in range(chips):
            acc_c[kk] += jnp.dot(
                xrow[source], dense[kk, part, :], preferred_element_type=f32
            )

    def all_to_rows():
        @pl.loop(0, k + 1)
        def _(j):
            kk = k - j
            mine = xcol.at[kk, pl.ds(q * rows, rows)]
            theirs = xcol.at[kk, pl.ds(other * rows, rows)]

            @pl.when(j > 0)
            def _():
                arrived(mine, plane_recv_sem.at[kk * CORES + q])
                to_sibling(kk, True)

            @pl.when(jnp.logical_or(j > 0, q == 1))
            def _():
                arrived(theirs, plane_recv_sem.at[kk * CORES + other])

            acc_r[...] += jnp.dot(dense[kk], xcol[kk], preferred_element_type=f32).reshape(
                acc_r.shape
            )

    def reduce_rows(t):
        def one(d, up, ahead, first, landing, recv_sem):
            @pl.when(both(ahead, first))
            def _():
                row_send[d] = acc_r[d].astype(bf16)

            @pl.when(both(ahead, jnp.logical_not(first)))
            def _():
                arrived(landing.at[d], recv_sem.at[d])
                row_send[d] = (acc_r[d] + landing[d].astype(f32)).astype(bf16)

            row_sum(d, up, True)

        up = n_col - 1 - t
        one(up, True, c < up, c == 0, row_up, up_recv_sem)
        one(t, False, c > t, c == n_col - 1, row_down, down_recv_sem)

    to_cols(c)

    @pl.loop(1, n_col)
    def _(s):
        low, high = c - s, c + s

        @pl.when(low >= 0)
        def _():
            arrived(xrow.at[low], gather_recv_sem.at[low])

        gather_up(low, True)

        @pl.when(high < n_col)
        def _():
            arrived(xrow.at[high], gather_recv_sem.at[high])

        gather_down(high, True)

        @pl.when(s == 1)
        def _():
            all_to_rows()

        @pl.loop(0, 2)
        def _(u):
            source = low + 2 * s * u

            @pl.when(both(source >= 0, source < n_col))
            def _():
                to_cols(source)

        @pl.when(s < n_col - 1)
        def _():
            reduce_rows(s - 1)

    here = pl.ds(pl.multiple_of(q * rows, rows), rows)
    there = pl.ds(pl.multiple_of(other * rows, rows), rows)

    @pl.loop(0, k + 1)
    def _(kk):
        sib_send[kk] = acc_c[kk, :, there].astype(bf16)
        pair(kk, True)

    reduce_rows(n_col - 2)

    @pl.loop(0, k)
    def _(kk):
        arrived(sib_recv.at[kk], pair_recv_sem.at[kk])
        col_send[kk] = (acc_c[kk, :, here] + sib_recv[kk].astype(f32)).astype(bf16)
        col_sum(kk).start()

    in_copy.wait()
    out_copy.wait()

    @pl.when(q == 0)
    def _():
        arrived(sib_recv.at[k], pair_recv_sem.at[k])
        acc_c[k, :, here] += sib_recv[k].astype(f32)

    @pl.when(c > 0)
    def _():
        arrived(row_up.at[c], up_recv_sem.at[c])
        acc_r[c] += row_up[c].astype(f32)

    @pl.when(c < n_col - 1)
    def _():
        arrived(row_down.at[c], down_recv_sem.at[c])
        acc_r[c] += row_down[c].astype(f32)

    @pl.loop(k + 1, chips)
    def _(kk):
        arrived(col_recv.at[kk], col_recv_sem.at[kk])
        acc_c[k, :, here] += col_recv[kk].astype(f32)

    combined = (x_ref[...].astype(f32) + acc_r[c] + acc_c[k, :, here].T).astype(bf16)
    hid = w_in.shape[1]
    part = min(hid, 256)
    total = jnp.zeros(out_ref.shape, f32) + bias_out_ref[...]
    for j in range(0, hid, part):
        hidden = jnp.dot(combined, w_in[:, j : j + part], preferred_element_type=f32)
        hidden = jnp.maximum(hidden + bias_in_ref[:, j : j + part], 0.0)
        total += jnp.dot(
            hidden.astype(bf16), w_out[j : j + part, :], preferred_element_type=f32
        )
    out_ref[...] = total.astype(bf16)

    gather_up(c, False)
    gather_down(c, False)
    to_sibling(k, False)
    for kk in range(1, chips):
        plane(kk, False)

    @pl.loop(1, n_col)
    def _(s):
        gather_up(c - s, False)
        gather_down(c + s, False)
        row_sum(n_col - s, True, False)
        row_sum(s - 1, False, False)

    @pl.loop(0, k)
    def _(kk):
        to_sibling(kk, False)
        pair(kk, False)
        col_sum(kk).wait_send()

    pair(k, False)


def solution(mesh):
    n_row = mesh.shape["row"]
    n_col = mesh.shape["col"]
    chips = n_row // CORES

    def shards(
        features, adjacency, tile_row, tile_column, tile_count, weight_in, bias_in, weight_out, bias_out
    ):
        rows, width = features.shape
        cap = adjacency.shape[1]
        blocks = rows // TILE
        places = n_row * n_col * blocks * blocks
        bf16, f32 = jnp.bfloat16, jnp.float32
        dma = pltpu.SemaphoreType.DMA
        vmem = pl.BlockSpec(memory_space=pltpu.VMEM)
        anywhere = pl.BlockSpec(memory_space=pl.ANY)
        scratch = [
            pltpu.VMEM((cap + 1, TILE, TILE), bf16),
            pltpu.VMEM((chips, n_col * rows, CORES * rows), bf16),
            pltpu.VMEM((8, -(-cap // TILE) * TILE), jnp.int32),
            pltpu.VMEM((1, places), jnp.int32),
            pltpu.SMEM((1, places), jnp.int32),
            pltpu.VMEM(weight_in.shape, bf16),
            pltpu.VMEM(weight_out.shape, bf16),
            pltpu.VMEM((chips, CORES * rows, width), bf16),
            pltpu.VMEM((n_col, width, rows), bf16),
            pltpu.VMEM((n_col, rows, width), f32),
            pltpu.VMEM((chips, width, CORES * rows), f32),
            pltpu.VMEM((n_col, rows, width), bf16),
            pltpu.VMEM((n_col, rows, width), bf16),
            pltpu.VMEM((n_col, rows, width), bf16),
            pltpu.VMEM((chips, width, rows), bf16),
            pltpu.VMEM((chips, width, rows), bf16),
            pltpu.VMEM((chips, width, rows), bf16),
            pltpu.VMEM((chips, width, rows), bf16),
            dma((4,)),
            dma((n_col,)),
            dma((n_col,)),
            dma((n_col,)),
            dma((chips,)),
            dma((n_row,)),
            dma((chips,)),
            dma((n_col,)),
            dma((n_col,)),
            dma((n_col,)),
            dma((n_col,)),
            dma((chips,)),
            dma((chips,)),
            dma((chips,)),
            dma((chips,)),
        ]
        return pl.pallas_call(
            functools.partial(kernel, n_row, n_col),
            out_shape=jax.ShapeDtypeStruct((rows, width), bf16),
            in_specs=[
                vmem,
                anywhere,
                vmem,
                vmem,
                pl.BlockSpec(memory_space=pltpu.SMEM),
                anywhere,
                vmem,
                anywhere,
                vmem,
            ],
            out_specs=vmem,
            scratch_shapes=scratch,
            compiler_params=pltpu.CompilerParams(
                collective_id=0, has_side_effects=True, vmem_limit_bytes=56 * 1024 * 1024
            ),
            name="gin_layer",
        )(
            features,
            adjacency,
            tile_row,
            tile_column,
            tile_count,
            weight_in,
            bias_in.reshape(1, -1),
            weight_out,
            bias_out.reshape(1, -1),
        )

    placed = (
        P(("row", "col"), None),
        P(("row", "col"), None, None, None),
        P(("row", "col"), None),
        P(("row", "col"), None),
        P(("row", "col")),
        P(),
        P(),
        P(),
        P(),
    )
    return jax.shard_map(
        shards, mesh=mesh, in_specs=placed, out_specs=P(("row", "col"), None), check_vma=False
    )
```

```python
import functools

import jax
import jax.numpy as jnp
from jax import lax
from jax.experimental import pallas as pl
from jax.experimental.pallas import tpu as pltpu
from jax.sharding import PartitionSpec as P

TILE = 128
CORES = 2
MESH = pl.DeviceIdType.MESH


def both(*conditions):
    result = conditions[0]
    for condition in conditions[1:]:
        result = jnp.logical_and(result, condition)
    return result


def kernel(
    n_row,
    n_col,
    x_ref,
    adjacency_ref,
    tile_row_ref,
    tile_column_ref,
    count_ref,
    weight_in_ref,
    bias_in_ref,
    weight_out_ref,
    bias_out_ref,
    out_ref,
    adj,
    dense,
    keys,
    slots_v,
    slots,
    w_in,
    w_out,
    xcol,
    xrow,
    acc_r,
    acc_c,
    row_send,
    row_up,
    row_down,
    sib_send,
    sib_recv,
    col_send,
    col_recv,
    local_sem,
    gather_up_sem,
    gather_down_sem,
    gather_recv_sem,
    plane_send_sem,
    plane_recv_sem,
    sibling_send_sem,
    up_send_sem,
    up_recv_sem,
    down_send_sem,
    down_recv_sem,
    pair_send_sem,
    pair_recv_sem,
    col_send_sem,
    col_recv_sem,
):
    _, width, rows = xrow.shape
    blocks = rows // TILE
    cap = adjacency_ref.shape[1]
    row_blocks = n_col * blocks
    col_blocks = n_row * blocks
    places = row_blocks * col_blocks
    chips = n_row // CORES
    wide = CORES * rows
    r = lax.axis_index("row")
    c = lax.axis_index("col")
    k = r // CORES
    q = r % CORES
    other = 1 - q
    sibling = (k * CORES + other, c)
    above = (r, c + 1)
    below = (r, c - 1)
    f32, bf16 = jnp.float32, jnp.bfloat16

    def remote(src, dst, send_sem, recv_sem, device):
        return pltpu.make_async_remote_copy(
            src_ref=src,
            dst_ref=dst,
            send_sem=send_sem,
            recv_sem=recv_sem,
            device_id=device,
            device_id_type=MESH,
        )

    def arrived(dst, sem):
        pltpu.make_async_copy(dst, dst, sem).wait()

    def run(condition, make, start):
        @pl.when(condition)
        def _():
            if start:
                make().start()
            else:
                make().wait_send()

    def gather_copy(b, up):
        sem = gather_up_sem if up else gather_down_sem
        device = above if up else below
        return remote(xrow.at[b], xrow.at[b], sem.at[b], gather_recv_sem.at[b], device)

    def gather_up(b, start):
        run(both(b >= 0, c < n_col - 1), lambda: gather_copy(b, True), start)

    def gather_down(b, start):
        run(both(b < n_col, c > 0), lambda: gather_copy(b, False), start)

    def plane(kk, start):
        run(
            kk > k,
            lambda: remote(
                xcol.at[k, pl.ds(q * rows, rows)],
                xcol.at[k, pl.ds(q * rows, rows)],
                plane_send_sem.at[kk],
                plane_recv_sem.at[r],
                (kk * CORES + q, c),
            ),
            start,
        )

    def to_sibling(kk, start):
        run(
            jnp.logical_or(kk < k, q == 0),
            lambda: remote(
                xcol.at[kk, pl.ds(q * rows, rows)],
                xcol.at[kk, pl.ds(q * rows, rows)],
                sibling_send_sem.at[kk],
                plane_recv_sem.at[kk * CORES + q],
                sibling,
            ),
            start,
        )

    def row_sum(d, up, start):
        run(
            both(c < d, d < n_col) if up else both(c > d, d >= 0),
            lambda: remote(
                row_send.at[d],
                (row_up if up else row_down).at[d],
                (up_send_sem if up else down_send_sem).at[d],
                (up_recv_sem if up else down_recv_sem).at[d],
                above if up else below,
            ),
            start,
        )

    def pair(kk, start):
        run(
            jnp.logical_or(kk < k, q == 1),
            lambda: remote(
                sib_send.at[kk],
                sib_recv.at[kk],
                pair_send_sem.at[kk],
                pair_recv_sem.at[kk],
                sibling,
            ),
            start,
        )

    def col_sum(kk):
        return remote(
            col_send.at[kk],
            col_recv.at[k],
            col_send_sem.at[kk],
            col_recv_sem.at[k],
            (kk * CORES + q, c),
        )

    barrier = pltpu.get_barrier_semaphore()
    pl.semaphore_signal(barrier, inc=1, device_id=sibling, device_id_type=MESH)
    for kk in range(chips):

        @pl.when(k != kk)
        def _():
            pl.semaphore_signal(
                barrier, inc=1, device_id=(kk * CORES + q, c), device_id_type=MESH
            )

    @pl.when(c > 0)
    def _():
        pl.semaphore_signal(barrier, inc=1, device_id=below, device_id_type=MESH)

    @pl.when(c < n_col - 1)
    def _():
        pl.semaphore_signal(barrier, inc=1, device_id=above, device_id_type=MESH)

    adj_copy = pltpu.make_async_copy(
        adjacency_ref.at[0], adj.at[pl.ds(0, cap)], local_sem.at[0]
    )
    adj_copy.start()
    in_copy = pltpu.make_async_copy(weight_in_ref, w_in, local_sem.at[1])
    in_copy.start()
    out_copy = pltpu.make_async_copy(weight_out_ref, w_out, local_sem.at[2])
    out_copy.start()

    xcol[k, pl.ds(pl.multiple_of(q * rows, rows), rows)] = x_ref[...]
    xrow[c] = x_ref[...].T

    lanes = keys.shape[1]
    keys[...] = jnp.full(keys.shape, -1, jnp.int32)
    slot_row = lax.broadcasted_iota(jnp.int32, (1, cap), 1)
    keys[0:1, 0:cap] = jnp.where(
        slot_row < count_ref[0],
        tile_row_ref[...] * col_blocks + tile_column_ref[...],
        -1,
    )
    key_column = jnp.broadcast_to(keys[0:1, :], (TILE, lanes)).T[:, 0:1]
    hit = key_column == lax.broadcasted_iota(jnp.int32, (lanes, places), 1)
    number = lax.broadcasted_iota(jnp.int32, (lanes, places), 0)
    slots_v[...] = cap + jnp.sum(
        jnp.where(hit, number - cap, 0), axis=0, keepdims=True
    )
    slot_copy = pltpu.make_async_copy(slots_v, slots, local_sem.at[3])
    slot_copy.start()
    adj[cap] = jnp.zeros((TILE, TILE), bf16)

    has_below = (c + n_col - 1) // n_col
    has_above = (2 * n_col - 2 - c) // n_col
    pl.semaphore_wait(barrier, chips + has_below + has_above)

    gather_up(c, True)
    gather_down(c, True)
    to_sibling(k, True)
    for kk in range(1, chips):
        plane(kk, True)

    @pl.when(q == 0)
    def _():
        xcol[k, pl.ds(rows, rows)] = jnp.zeros((rows, width), bf16)

    acc_r[...] = jnp.zeros(acc_r.shape, f32)
    acc_c[...] = jnp.zeros(acc_c.shape, f32)
    slot_copy.wait()
    adj_copy.wait()

    @pl.loop(0, chips)
    def _(kk):
        for i in range(row_blocks):
            for b in range(CORES * blocks):
                place = i * col_blocks + kk * (CORES * blocks) + b
                dense[kk, pl.ds(i * TILE, TILE), pl.ds(b * TILE, TILE)] = adj[
                    slots[0, place]
                ]

    def to_cols(source):
        part = pl.ds(pl.multiple_of(source * rows, rows), rows)
        for kk in range(chips):
            acc_c[kk] += jnp.dot(
                xrow[source], dense[kk, part, :], preferred_element_type=f32
            )

    def rows_step(j):
        @pl.when(j <= k)
        def _():
            kk = k - j
            mine = xcol.at[kk, pl.ds(q * rows, rows)]
            theirs = xcol.at[kk, pl.ds(other * rows, rows)]

            @pl.when(j > 0)
            def _():
                arrived(mine, plane_recv_sem.at[kk * CORES + q])
                to_sibling(kk, True)

            @pl.when(jnp.logical_or(j > 0, q == 1))
            def _():
                arrived(theirs, plane_recv_sem.at[kk * CORES + other])

            acc_r[...] += jnp.dot(dense[kk], xcol[kk], preferred_element_type=f32).reshape(
                acc_r.shape
            )

    def gather_step(s):
        low, high = c - s, c + s

        @pl.when(low >= 0)
        def _():
            arrived(xrow.at[low], gather_recv_sem.at[low])

        gather_up(low, True)

        @pl.when(high < n_col)
        def _():
            arrived(xrow.at[high], gather_recv_sem.at[high])

        gather_down(high, True)

    def cols_step(s):
        @pl.loop(0, 2)
        def _(u):
            source = c - s + 2 * s * u

            @pl.when(both(source >= 0, source < n_col))
            def _():
                to_cols(source)

    def reduce_rows(t):
        def one(d, up, ahead, first, landing, recv_sem):
            @pl.when(both(ahead, first))
            def _():
                row_send[d] = acc_r[d].astype(bf16)

            @pl.when(both(ahead, jnp.logical_not(first)))
            def _():
                arrived(landing.at[d], recv_sem.at[d])
                row_send[d] = (acc_r[d] + landing[d].astype(f32)).astype(bf16)

            row_sum(d, up, True)

        up = n_col - 1 - t + c
        down = t - (n_col - 1) + c
        one(up, True, both(c < up, up < n_col), c == 0, row_up, up_recv_sem)
        one(down, False, both(c > down, down >= 0), c == n_col - 1, row_down, down_recv_sem)

    to_cols(c)

    @pl.loop(0, max(chips, n_col - 1))
    def _(j):
        rows_step(j)

        @pl.when(j < n_col - 2)
        def _():
            gather_step(j + 1)

    reduce_rows(0)

    @pl.loop(1, n_col - 1)
    def _(s):
        cols_step(s)

    gather_step(n_col - 1)
    cols_step(n_col - 1)

    here = pl.ds(pl.multiple_of(q * rows, rows), rows)
    there = pl.ds(pl.multiple_of(other * rows, rows), rows)

    @pl.loop(0, k + 1)
    def _(kk):
        sib_send[kk] = acc_c[kk, :, there].astype(bf16)
        pair(kk, True)

    @pl.loop(0, k)
    def _(kk):
        arrived(sib_recv.at[kk], pair_recv_sem.at[kk])
        col_send[kk] = (acc_c[kk, :, here] + sib_recv[kk].astype(f32)).astype(bf16)
        col_sum(kk).start()

    @pl.loop(1, n_col - 1)
    def _(t):
        reduce_rows(t)

    in_copy.wait()
    out_copy.wait()

    @pl.when(q == 0)
    def _():
        arrived(sib_recv.at[k], pair_recv_sem.at[k])
        acc_c[k, :, here] += sib_recv[k].astype(f32)

    @pl.when(c > 0)
    def _():
        arrived(row_up.at[c], up_recv_sem.at[c])
        acc_r[c] += row_up[c].astype(f32)

    @pl.when(c < n_col - 1)
    def _():
        arrived(row_down.at[c], down_recv_sem.at[c])
        acc_r[c] += row_down[c].astype(f32)

    @pl.loop(k + 1, chips)
    def _(kk):
        arrived(col_recv.at[kk], col_recv_sem.at[kk])
        acc_c[k, :, here] += col_recv[kk].astype(f32)

    combined = (x_ref[...].astype(f32) + acc_r[c] + acc_c[k, :, here].T).astype(bf16)
    hid = w_in.shape[1]
    part = min(hid, 256)
    total = jnp.zeros(out_ref.shape, f32) + bias_out_ref[...]
    for j in range(0, hid, part):
        hidden = jnp.dot(combined, w_in[:, j : j + part], preferred_element_type=f32)
        hidden = jnp.maximum(hidden + bias_in_ref[:, j : j + part], 0.0)
        total += jnp.dot(
            hidden.astype(bf16), w_out[j : j + part, :], preferred_element_type=f32
        )
    out_ref[...] = total.astype(bf16)

    gather_up(c, False)
    gather_down(c, False)
    to_sibling(k, False)
    for kk in range(1, chips):
        plane(kk, False)

    @pl.loop(1, n_col)
    def _(s):
        gather_up(c - s, False)
        gather_down(c + s, False)
        row_sum(n_col - s, True, False)
        row_sum(s - 1, False, False)

    @pl.loop(0, k)
    def _(kk):
        to_sibling(kk, False)
        pair(kk, False)
        col_sum(kk).wait_send()

    pair(k, False)


def solution(mesh):
    n_row = mesh.shape["row"]
    n_col = mesh.shape["col"]
    chips = n_row // CORES

    def shards(
        features, adjacency, tile_row, tile_column, tile_count, weight_in, bias_in, weight_out, bias_out
    ):
        rows, width = features.shape
        cap = adjacency.shape[1]
        blocks = rows // TILE
        places = n_row * n_col * blocks * blocks
        bf16, f32 = jnp.bfloat16, jnp.float32
        dma = pltpu.SemaphoreType.DMA
        vmem = pl.BlockSpec(memory_space=pltpu.VMEM)
        anywhere = pl.BlockSpec(memory_space=pl.ANY)
        scratch = [
            pltpu.VMEM((cap + 1, TILE, TILE), bf16),
            pltpu.VMEM((chips, n_col * rows, CORES * rows), bf16),
            pltpu.VMEM((8, -(-cap // TILE) * TILE), jnp.int32),
            pltpu.VMEM((1, places), jnp.int32),
            pltpu.SMEM((1, places), jnp.int32),
            pltpu.VMEM(weight_in.shape, bf16),
            pltpu.VMEM(weight_out.shape, bf16),
            pltpu.VMEM((chips, CORES * rows, width), bf16),
            pltpu.VMEM((n_col, width, rows), bf16),
            pltpu.VMEM((n_col, rows, width), f32),
            pltpu.VMEM((chips, width, CORES * rows), f32),
            pltpu.VMEM((n_col, rows, width), bf16),
            pltpu.VMEM((n_col, rows, width), bf16),
            pltpu.VMEM((n_col, rows, width), bf16),
            pltpu.VMEM((chips, width, rows), bf16),
            pltpu.VMEM((chips, width, rows), bf16),
            pltpu.VMEM((chips, width, rows), bf16),
            pltpu.VMEM((chips, width, rows), bf16),
            dma((4,)),
            dma((n_col,)),
            dma((n_col,)),
            dma((n_col,)),
            dma((chips,)),
            dma((n_row,)),
            dma((chips,)),
            dma((n_col,)),
            dma((n_col,)),
            dma((n_col,)),
            dma((n_col,)),
            dma((chips,)),
            dma((chips,)),
            dma((chips,)),
            dma((chips,)),
        ]
        return pl.pallas_call(
            functools.partial(kernel, n_row, n_col),
            out_shape=jax.ShapeDtypeStruct((rows, width), bf16),
            in_specs=[
                vmem,
                anywhere,
                vmem,
                vmem,
                pl.BlockSpec(memory_space=pltpu.SMEM),
                anywhere,
                vmem,
                anywhere,
                vmem,
            ],
            out_specs=vmem,
            scratch_shapes=scratch,
            compiler_params=pltpu.CompilerParams(
                collective_id=0, has_side_effects=True, vmem_limit_bytes=56 * 1024 * 1024
            ),
            name="gin_layer",
        )(
            features,
            adjacency,
            tile_row,
            tile_column,
            tile_count,
            weight_in,
            bias_in.reshape(1, -1),
            weight_out,
            bias_out.reshape(1, -1),
        )

    placed = (
        P(("row", "col"), None),
        P(("row", "col"), None, None, None),
        P(("row", "col"), None),
        P(("row", "col"), None),
        P(("row", "col")),
        P(),
        P(),
        P(),
        P(),
    )
    return jax.shard_map(
        shards, mesh=mesh, in_specs=placed, out_specs=P(("row", "col"), None), check_vma=False
    )
```

```python
import functools

import jax
import jax.numpy as jnp
from jax import lax
from jax.experimental import pallas as pl
from jax.experimental.pallas import tpu as pltpu
from jax.sharding import PartitionSpec as P

TILE = 128
CORES = 2
CHUNKS = 2
MESH = pl.DeviceIdType.MESH


def both(*conditions):
    result = conditions[0]
    for condition in conditions[1:]:
        result = jnp.logical_and(result, condition)
    return result


def kernel(
    n_row,
    n_col,
    x_ref,
    adjacency_ref,
    tile_row_ref,
    tile_column_ref,
    count_ref,
    weight_in_ref,
    bias_in_ref,
    weight_out_ref,
    bias_out_ref,
    out_ref,
    adj,
    dense,
    keys,
    slots_v,
    slots,
    w_in,
    w_out,
    xcol,
    xrow,
    acc_r,
    acc_c,
    row_send,
    row_up,
    row_down,
    sib_send,
    sib_recv,
    col_send,
    col_recv,
    combined_ref,
    local_sem,
    gather_up_sem,
    gather_down_sem,
    gather_recv_sem,
    plane_send_sem,
    plane_recv_sem,
    sibling_send_sem,
    up_send_sem,
    up_recv_sem,
    down_send_sem,
    down_recv_sem,
    pair_send_sem,
    pair_recv_sem,
    col_send_sem,
    col_recv_sem,
):
    chunks, _, fw, rows = xrow.shape
    blocks = rows // TILE
    cap = adjacency_ref.shape[1]
    row_blocks = n_col * blocks
    col_blocks = n_row * blocks
    places = row_blocks * col_blocks
    chips = n_row // CORES
    wide = CORES * rows
    r = lax.axis_index("row")
    c = lax.axis_index("col")
    k = r // CORES
    q = r % CORES
    other = 1 - q
    sibling = (k * CORES + other, c)
    above = (r, c + 1)
    below = (r, c - 1)
    f32, bf16 = jnp.float32, jnp.bfloat16

    def remote(src, dst, send_sem, recv_sem, device):
        return pltpu.make_async_remote_copy(
            src_ref=src,
            dst_ref=dst,
            send_sem=send_sem,
            recv_sem=recv_sem,
            device_id=device,
            device_id_type=MESH,
        )

    def arrived(dst, sem):
        pltpu.make_async_copy(dst, dst, sem).wait()

    def run(condition, make, start):
        @pl.when(condition)
        def _():
            if start:
                make().start()
            else:
                make().wait_send()

    def gather_copy(h, b, up):
        sem = gather_up_sem if up else gather_down_sem
        device = above if up else below
        return remote(xrow.at[h, b], xrow.at[h, b], sem.at[h, b], gather_recv_sem.at[h, b], device)

    def gather_up(h, b, start):
        run(both(b >= 0, c < n_col - 1), lambda: gather_copy(h, b, True), start)

    def gather_down(h, b, start):
        run(both(b < n_col, c > 0), lambda: gather_copy(h, b, False), start)

    def plane(h, kk, start):
        run(
            kk > k,
            lambda: remote(
                xcol.at[h, k, pl.ds(q * rows, rows)],
                xcol.at[h, k, pl.ds(q * rows, rows)],
                plane_send_sem.at[h, kk],
                plane_recv_sem.at[h, r],
                (kk * CORES + q, c),
            ),
            start,
        )

    def to_sibling(h, kk, start):
        run(
            jnp.logical_or(kk < k, q == 0),
            lambda: remote(
                xcol.at[h, kk, pl.ds(q * rows, rows)],
                xcol.at[h, kk, pl.ds(q * rows, rows)],
                sibling_send_sem.at[h, kk],
                plane_recv_sem.at[h, kk * CORES + q],
                sibling,
            ),
            start,
        )

    def row_sum(h, d, up, start):
        run(
            both(c < d, d < n_col) if up else both(c > d, d >= 0),
            lambda: remote(
                row_send.at[h, d],
                (row_up if up else row_down).at[h, d],
                (up_send_sem if up else down_send_sem).at[h, d],
                (up_recv_sem if up else down_recv_sem).at[h, d],
                above if up else below,
            ),
            start,
        )

    def pair(h, kk, start):
        run(
            jnp.logical_or(kk < k, q == 1),
            lambda: remote(
                sib_send.at[h, kk],
                sib_recv.at[h, kk],
                pair_send_sem.at[h, kk],
                pair_recv_sem.at[h, kk],
                sibling,
            ),
            start,
        )

    def col_sum(h, kk):
        return remote(
            col_send.at[h, kk],
            col_recv.at[h, k],
            col_send_sem.at[h, kk],
            col_recv_sem.at[h, k],
            (kk * CORES + q, c),
        )

    barrier = pltpu.get_barrier_semaphore()
    pl.semaphore_signal(barrier, inc=1, device_id=sibling, device_id_type=MESH)
    for kk in range(chips):

        @pl.when(k != kk)
        def _():
            pl.semaphore_signal(
                barrier, inc=1, device_id=(kk * CORES + q, c), device_id_type=MESH
            )

    @pl.when(c > 0)
    def _():
        pl.semaphore_signal(barrier, inc=1, device_id=below, device_id_type=MESH)

    @pl.when(c < n_col - 1)
    def _():
        pl.semaphore_signal(barrier, inc=1, device_id=above, device_id_type=MESH)

    adj_copy = pltpu.make_async_copy(
        adjacency_ref.at[0], adj.at[pl.ds(0, cap)], local_sem.at[0]
    )
    adj_copy.start()
    in_copy = pltpu.make_async_copy(weight_in_ref, w_in, local_sem.at[1])
    in_copy.start()
    out_copy = pltpu.make_async_copy(weight_out_ref, w_out, local_sem.at[2])
    out_copy.start()

    here = pl.ds(pl.multiple_of(q * rows, rows), rows)
    there = pl.ds(pl.multiple_of(other * rows, rows), rows)
    for h in range(chunks):
        own = x_ref[:, h * fw : (h + 1) * fw]
        xcol[h, k, here] = own
        xrow[h, c] = own.T

    has_below = (c + n_col - 1) // n_col
    has_above = (2 * n_col - 2 - c) // n_col
    pl.semaphore_wait(barrier, chips + has_below + has_above)

    for h in range(chunks):
        gather_up(h, c, True)
        gather_down(h, c, True)
        for kk in range(1, chips):
            plane(h, kk, True)
        to_sibling(h, k, True)

        @pl.when(q == 0)
        def _():
            xcol[h, k, pl.ds(rows, rows)] = jnp.zeros((rows, fw), bf16)

    lanes = keys.shape[1]
    keys[...] = jnp.full(keys.shape, -1, jnp.int32)
    slot_row = lax.broadcasted_iota(jnp.int32, (1, cap), 1)
    keys[0:1, 0:cap] = jnp.where(
        slot_row < count_ref[0],
        tile_row_ref[...] * col_blocks + tile_column_ref[...],
        -1,
    )
    key_column = jnp.broadcast_to(keys[0:1, :], (TILE, lanes)).T[:, 0:1]
    hit = key_column == lax.broadcasted_iota(jnp.int32, (lanes, places), 1)
    number = lax.broadcasted_iota(jnp.int32, (lanes, places), 0)
    slots_v[...] = cap + jnp.sum(
        jnp.where(hit, number - cap, 0), axis=0, keepdims=True
    )
    slot_copy = pltpu.make_async_copy(slots_v, slots, local_sem.at[3])
    slot_copy.start()
    adj[cap] = jnp.zeros((TILE, TILE), bf16)

    acc_r[...] = jnp.zeros(acc_r.shape, f32)
    acc_c[...] = jnp.zeros(acc_c.shape, f32)
    slot_copy.wait()
    adj_copy.wait()

    @pl.loop(0, chips)
    def _(kk):
        for i in range(row_blocks):
            for b in range(CORES * blocks):
                place = i * col_blocks + kk * (CORES * blocks) + b
                dense[kk, pl.ds(i * TILE, TILE), pl.ds(b * TILE, TILE)] = adj[
                    slots[0, place]
                ]

    def to_cols(h, source):
        part = pl.ds(pl.multiple_of(source * rows, rows), rows)
        for kk in range(chips):
            acc_c[h, kk] += jnp.dot(
                xrow[h, source], dense[kk, part, :], preferred_element_type=f32
            )

    def rows_step(h, j):
        @pl.when(j <= k)
        def _():
            kk = k - j
            mine = xcol.at[h, kk, pl.ds(q * rows, rows)]
            theirs = xcol.at[h, kk, pl.ds(other * rows, rows)]

            @pl.when(j > 0)
            def _():
                arrived(mine, plane_recv_sem.at[h, kk * CORES + q])
                to_sibling(h, kk, True)

            @pl.when(jnp.logical_or(j > 0, q == 1))
            def _():
                arrived(theirs, plane_recv_sem.at[h, kk * CORES + other])

            acc_r[h] += jnp.dot(
                dense[kk], xcol[h, kk], preferred_element_type=f32
            ).reshape(n_col, rows, fw)

    def gather_step(h, s):
        low, high = c - s, c + s

        @pl.when(low >= 0)
        def _():
            arrived(xrow.at[h, low], gather_recv_sem.at[h, low])

        gather_up(h, low, True)

        @pl.when(high < n_col)
        def _():
            arrived(xrow.at[h, high], gather_recv_sem.at[h, high])

        gather_down(h, high, True)

    def cols_step(h, s):
        @pl.loop(0, 2)
        def _(u):
            source = c - s + 2 * s * u

            @pl.when(both(source >= 0, source < n_col))
            def _():
                to_cols(h, source)

    def reduce_rows(h, t):
        def one(d, up, ahead, first, landing, recv_sem):
            @pl.when(both(ahead, first))
            def _():
                row_send[h, d] = acc_r[h, d].astype(bf16)

            @pl.when(both(ahead, jnp.logical_not(first)))
            def _():
                arrived(landing.at[h, d], recv_sem.at[h, d])
                row_send[h, d] = (acc_r[h, d] + landing[h, d].astype(f32)).astype(bf16)

            row_sum(h, d, up, True)

        up = n_col - 1 - t + c
        down = t - (n_col - 1) + c
        one(up, True, both(c < up, up < n_col), c == 0, row_up, up_recv_sem)
        one(down, False, both(c > down, down >= 0), c == n_col - 1, row_down, down_recv_sem)

    def pair_start(h):
        @pl.loop(0, k + 1)
        def _(kk):
            sib_send[h, kk] = acc_c[h, kk, :, there].astype(bf16)
            pair(h, kk, True)

    def reduce_cols(h):
        @pl.loop(0, k)
        def _(kk):
            arrived(sib_recv.at[h, kk], pair_recv_sem.at[h, kk])
            col_send[h, kk] = (
                acc_c[h, kk, :, here] + sib_recv[h, kk].astype(f32)
            ).astype(bf16)
            col_sum(h, kk).start()

    def finish(h):
        @pl.when(q == 0)
        def _():
            arrived(sib_recv.at[h, k], pair_recv_sem.at[h, k])
            acc_c[h, k, :, here] += sib_recv[h, k].astype(f32)

        @pl.loop(k + 1, chips)
        def _(kk):
            arrived(col_recv.at[h, kk], col_recv_sem.at[h, kk])
            acc_c[h, k, :, here] += col_recv[h, kk].astype(f32)

        @pl.when(c > 0)
        def _():
            arrived(row_up.at[h, c], up_recv_sem.at[h, c])
            acc_r[h, c] += row_up[h, c].astype(f32)

        @pl.when(c < n_col - 1)
        def _():
            arrived(row_down.at[h, c], down_recv_sem.at[h, c])
            acc_r[h, c] += row_down[h, c].astype(f32)

        own = x_ref[:, h * fw : (h + 1) * fw].astype(f32)
        combined_ref[:, h * fw : (h + 1) * fw] = (
            own + acc_r[h, c] + acc_c[h, k, :, here].T
        ).astype(bf16)

    last = n_col - 1
    for h in range(chunks):
        to_cols(h, c)
    for h in range(chunks):

        @pl.loop(0, max(chips, last))
        def _(j):
            rows_step(h, j)
            if h == 0:

                @pl.when(j < last - 1)
                def _():
                    for g in range(chunks):
                        gather_step(g, j + 1)

        reduce_rows(h, 0)
        if h == 0:

            @pl.loop(1, last)
            def _(s):
                cols_step(0, s)

    for h in range(chunks):
        if h > 0:

            @pl.loop(1, last)
            def _(s):
                cols_step(h, s)

        gather_step(h, last)
        cols_step(h, last)
        pair_start(h)
        reduce_rows(h, 1)
        if h < chunks - 1:
            reduce_cols(h)

    @pl.loop(2, last)
    def _(t):
        for h in range(chunks - 1):
            reduce_rows(h, t)

    reduce_cols(chunks - 1)

    @pl.loop(2, last)
    def _(t):
        reduce_rows(chunks - 1, t)

    in_copy.wait()
    out_copy.wait()
    for h in range(chunks):
        finish(h)

    combined = combined_ref[...]
    hid = w_in.shape[1]
    part = min(hid, 256)
    total = jnp.zeros(out_ref.shape, f32) + bias_out_ref[...]
    for j in range(0, hid, part):
        hidden = jnp.dot(combined, w_in[:, j : j + part], preferred_element_type=f32)
        hidden = jnp.maximum(hidden + bias_in_ref[:, j : j + part], 0.0)
        total += jnp.dot(
            hidden.astype(bf16), w_out[j : j + part, :], preferred_element_type=f32
        )
    out_ref[...] = total.astype(bf16)

    for h in range(chunks):
        gather_up(h, c, False)
        gather_down(h, c, False)
        to_sibling(h, k, False)
        for kk in range(1, chips):
            plane(h, kk, False)

        @pl.loop(1, n_col)
        def _(s):
            gather_up(h, c - s, False)
            gather_down(h, c + s, False)
            row_sum(h, n_col - s, True, False)
            row_sum(h, s - 1, False, False)

        @pl.loop(0, k)
        def _(kk):
            to_sibling(h, kk, False)
            pair(h, kk, False)
            col_sum(h, kk).wait_send()

        pair(h, k, False)


def solution(mesh):
    n_row = mesh.shape["row"]
    n_col = mesh.shape["col"]
    chips = n_row // CORES

    def shards(
        features, adjacency, tile_row, tile_column, tile_count, weight_in, bias_in, weight_out, bias_out
    ):
        rows, width = features.shape
        fw = width // CHUNKS
        cap = adjacency.shape[1]
        blocks = rows // TILE
        places = n_row * n_col * blocks * blocks
        bf16, f32 = jnp.bfloat16, jnp.float32
        dma = pltpu.SemaphoreType.DMA
        vmem = pl.BlockSpec(memory_space=pltpu.VMEM)
        anywhere = pl.BlockSpec(memory_space=pl.ANY)
        scratch = [
            pltpu.VMEM((cap + 1, TILE, TILE), bf16),
            pltpu.VMEM((chips, n_col * rows, CORES * rows), bf16),
            pltpu.VMEM((8, -(-cap // TILE) * TILE), jnp.int32),
            pltpu.VMEM((1, places), jnp.int32),
            pltpu.SMEM((1, places), jnp.int32),
            pltpu.VMEM(weight_in.shape, bf16),
            pltpu.VMEM(weight_out.shape, bf16),
            pltpu.VMEM((CHUNKS, chips, CORES * rows, fw), bf16),
            pltpu.VMEM((CHUNKS, n_col, fw, rows), bf16),
            pltpu.VMEM((CHUNKS, n_col, rows, fw), f32),
            pltpu.VMEM((CHUNKS, chips, fw, CORES * rows), f32),
            pltpu.VMEM((CHUNKS, n_col, rows, fw), bf16),
            pltpu.VMEM((CHUNKS, n_col, rows, fw), bf16),
            pltpu.VMEM((CHUNKS, n_col, rows, fw), bf16),
            pltpu.VMEM((CHUNKS, chips, fw, rows), bf16),
            pltpu.VMEM((CHUNKS, chips, fw, rows), bf16),
            pltpu.VMEM((CHUNKS, chips, fw, rows), bf16),
            pltpu.VMEM((CHUNKS, chips, fw, rows), bf16),
            pltpu.VMEM((rows, width), bf16),
            dma((4,)),
            dma((CHUNKS, n_col)),
            dma((CHUNKS, n_col)),
            dma((CHUNKS, n_col)),
            dma((CHUNKS, chips)),
            dma((CHUNKS, n_row)),
            dma((CHUNKS, chips)),
            dma((CHUNKS, n_col)),
            dma((CHUNKS, n_col)),
            dma((CHUNKS, n_col)),
            dma((CHUNKS, n_col)),
            dma((CHUNKS, chips)),
            dma((CHUNKS, chips)),
            dma((CHUNKS, chips)),
            dma((CHUNKS, chips)),
        ]
        return pl.pallas_call(
            functools.partial(kernel, n_row, n_col),
            out_shape=jax.ShapeDtypeStruct((rows, width), bf16),
            in_specs=[
                vmem,
                anywhere,
                vmem,
                vmem,
                pl.BlockSpec(memory_space=pltpu.SMEM),
                anywhere,
                vmem,
                anywhere,
                vmem,
            ],
            out_specs=vmem,
            scratch_shapes=scratch,
            compiler_params=pltpu.CompilerParams(
                collective_id=0, has_side_effects=True, vmem_limit_bytes=56 * 1024 * 1024
            ),
            name="gin_layer",
        )(
            features,
            adjacency,
            tile_row,
            tile_column,
            tile_count,
            weight_in,
            bias_in.reshape(1, -1),
            weight_out,
            bias_out.reshape(1, -1),
        )

    placed = (
        P(("row", "col"), None),
        P(("row", "col"), None, None, None),
        P(("row", "col"), None),
        P(("row", "col"), None),
        P(("row", "col")),
        P(),
        P(),
        P(),
        P(),
    )
    return jax.shard_map(
        shards, mesh=mesh, in_specs=placed, out_specs=P(("row", "col"), None), check_vma=False
    )
```

```python
import functools

import jax
import jax.numpy as jnp
from jax import lax
from jax.experimental import pallas as pl
from jax.experimental.pallas import tpu as pltpu
from jax.sharding import PartitionSpec as P

TILE = 128
CORES = 2
MESH = pl.DeviceIdType.MESH


def both(*conditions):
    result = conditions[0]
    for condition in conditions[1:]:
        result = jnp.logical_and(result, condition)
    return result


def kernel(
    n_row,
    n_col,
    x_ref,
    adjacency_ref,
    tile_row_ref,
    tile_column_ref,
    count_ref,
    weight_in_ref,
    bias_in_ref,
    weight_out_ref,
    bias_out_ref,
    out_ref,
    adj,
    dense,
    keys,
    slots_v,
    slots,
    w_in,
    w_out,
    xcol,
    xrow,
    acc_r,
    acc_c,
    row_send,
    row_up,
    row_down,
    sib_send,
    sib_recv,
    col_send,
    col_recv,
    local_sem,
    gather_up_sem,
    gather_down_sem,
    gather_recv_sem,
    plane_send_sem,
    plane_recv_sem,
    sibling_send_sem,
    up_send_sem,
    up_recv_sem,
    down_send_sem,
    down_recv_sem,
    pair_send_sem,
    pair_recv_sem,
    col_send_sem,
    col_recv_sem,
):
    _, width, rows = xrow.shape
    blocks = rows // TILE
    cap = adjacency_ref.shape[1]
    row_blocks = n_col * blocks
    col_blocks = n_row * blocks
    places = row_blocks * col_blocks
    chips = n_row // CORES
    wide = CORES * rows
    r = lax.axis_index("row")
    c = lax.axis_index("col")
    k = r // CORES
    q = r % CORES
    other = 1 - q
    sibling = (k * CORES + other, c)
    above = (r, c + 1)
    below = (r, c - 1)
    f32, bf16 = jnp.float32, jnp.bfloat16

    def remote(src, dst, send_sem, recv_sem, device):
        return pltpu.make_async_remote_copy(
            src_ref=src,
            dst_ref=dst,
            send_sem=send_sem,
            recv_sem=recv_sem,
            device_id=device,
            device_id_type=MESH,
        )

    def arrived(dst, sem):
        pltpu.make_async_copy(dst, dst, sem).wait()

    def run(condition, make, start):
        @pl.when(condition)
        def _():
            if start:
                make().start()
            else:
                make().wait_send()

    def gather_copy(b, up):
        sem = gather_up_sem if up else gather_down_sem
        device = above if up else below
        return remote(xrow.at[b], xrow.at[b], sem.at[b], gather_recv_sem.at[b], device)

    def gather_up(b, start):
        run(both(b >= 0, c < n_col - 1), lambda: gather_copy(b, True), start)

    def gather_down(b, start):
        run(both(b < n_col, c > 0), lambda: gather_copy(b, False), start)

    def plane(kk, start):
        run(
            kk > k,
            lambda: remote(
                xcol.at[k, pl.ds(q * rows, rows)],
                xcol.at[k, pl.ds(q * rows, rows)],
                plane_send_sem.at[kk],
                plane_recv_sem.at[r],
                (kk * CORES + q, c),
            ),
            start,
        )

    def to_sibling(kk, start):
        run(
            jnp.logical_or(kk < k, q == 0),
            lambda: remote(
                xcol.at[kk, pl.ds(q * rows, rows)],
                xcol.at[kk, pl.ds(q * rows, rows)],
                sibling_send_sem.at[kk],
                plane_recv_sem.at[kk * CORES + q],
                sibling,
            ),
            start,
        )

    def row_sum(d, up, start):
        run(
            both(c < d, d < n_col) if up else both(c > d, d >= 0),
            lambda: remote(
                row_send.at[d],
                (row_up if up else row_down).at[d],
                (up_send_sem if up else down_send_sem).at[d],
                (up_recv_sem if up else down_recv_sem).at[d],
                above if up else below,
            ),
            start,
        )

    def pair(kk, start):
        run(
            jnp.logical_or(kk < k, q == 1),
            lambda: remote(
                sib_send.at[kk],
                sib_recv.at[kk],
                pair_send_sem.at[kk],
                pair_recv_sem.at[kk],
                sibling,
            ),
            start,
        )

    def col_sum(kk):
        return remote(
            col_send.at[kk],
            col_recv.at[k],
            col_send_sem.at[kk],
            col_recv_sem.at[k],
            (kk * CORES + q, c),
        )

    barrier = pltpu.get_barrier_semaphore()
    pl.semaphore_signal(barrier, inc=1, device_id=sibling, device_id_type=MESH)
    for kk in range(chips):

        @pl.when(k != kk)
        def _():
            pl.semaphore_signal(
                barrier, inc=1, device_id=(kk * CORES + q, c), device_id_type=MESH
            )

    @pl.when(c > 0)
    def _():
        pl.semaphore_signal(barrier, inc=1, device_id=below, device_id_type=MESH)

    @pl.when(c < n_col - 1)
    def _():
        pl.semaphore_signal(barrier, inc=1, device_id=above, device_id_type=MESH)

    adj_copy = pltpu.make_async_copy(
        adjacency_ref.at[0], adj.at[pl.ds(0, cap)], local_sem.at[0]
    )
    adj_copy.start()
    in_copy = pltpu.make_async_copy(weight_in_ref, w_in, local_sem.at[1])
    in_copy.start()
    out_copy = pltpu.make_async_copy(weight_out_ref, w_out, local_sem.at[2])
    out_copy.start()

    xcol[k, pl.ds(pl.multiple_of(q * rows, rows), rows)] = x_ref[...]
    xrow[c] = x_ref[...].T

    has_below = (c + n_col - 1) // n_col
    has_above = (2 * n_col - 2 - c) // n_col
    pl.semaphore_wait(barrier, chips + has_below + has_above)

    gather_up(c, True)
    gather_down(c, True)
    to_sibling(k, True)
    for kk in range(1, chips):
        plane(kk, True)

    @pl.when(q == 0)
    def _():
        xcol[k, pl.ds(rows, rows)] = jnp.zeros((rows, width), bf16)

    lanes = keys.shape[1]
    keys[...] = jnp.full(keys.shape, -1, jnp.int32)
    slot_row = lax.broadcasted_iota(jnp.int32, (1, cap), 1)
    keys[0:1, 0:cap] = jnp.where(
        slot_row < count_ref[0],
        tile_row_ref[...] * col_blocks + tile_column_ref[...],
        -1,
    )
    key_column = jnp.broadcast_to(keys[0:1, :], (TILE, lanes)).T[:, 0:1]
    hit = key_column == lax.broadcasted_iota(jnp.int32, (lanes, places), 1)
    number = lax.broadcasted_iota(jnp.int32, (lanes, places), 0)
    slots_v[...] = cap + jnp.sum(
        jnp.where(hit, number - cap, 0), axis=0, keepdims=True
    )
    slot_copy = pltpu.make_async_copy(slots_v, slots, local_sem.at[3])
    slot_copy.start()
    adj[cap] = jnp.zeros((TILE, TILE), bf16)

    slot_copy.wait()
    adj_copy.wait()

    @pl.loop(0, chips)
    def _(kk):
        for i in range(row_blocks):
            for b in range(CORES * blocks):
                place = i * col_blocks + kk * (CORES * blocks) + b
                dense[kk, pl.ds(i * TILE, TILE), pl.ds(b * TILE, TILE)] = adj[
                    slots[0, place]
                ]

    def to_cols(source, first=False):
        part = pl.ds(pl.multiple_of(source * rows, rows), rows)
        for kk in range(chips):
            added = jnp.dot(xrow[source], dense[kk, part, :], preferred_element_type=f32)
            acc_c[kk] = added if first else acc_c[kk] + added

    def rows_step(j, first=False):
        @pl.when(j <= k)
        def _():
            kk = k - j
            mine = xcol.at[kk, pl.ds(q * rows, rows)]
            theirs = xcol.at[kk, pl.ds(other * rows, rows)]

            @pl.when(j > 0)
            def _():
                arrived(mine, plane_recv_sem.at[kk * CORES + q])
                to_sibling(kk, True)

            @pl.when(jnp.logical_or(j > 0, q == 1))
            def _():
                arrived(theirs, plane_recv_sem.at[kk * CORES + other])

            added = jnp.dot(dense[kk], xcol[kk], preferred_element_type=f32)
            added = added.reshape(acc_r.shape)
            acc_r[...] = added if first else acc_r[...] + added

    def gather_step(s):
        low, high = c - s, c + s

        @pl.when(low >= 0)
        def _():
            arrived(xrow.at[low], gather_recv_sem.at[low])

        gather_up(low, True)

        @pl.when(high < n_col)
        def _():
            arrived(xrow.at[high], gather_recv_sem.at[high])

        gather_down(high, True)

    def cols_step(s):
        @pl.loop(0, 2)
        def _(u):
            source = c - s + 2 * s * u

            @pl.when(both(source >= 0, source < n_col))
            def _():
                to_cols(source)

    def start_rows():
        @pl.when(c == 0)
        def _():
            @pl.loop(1, n_col)
            def _(s):
                row_send[n_col - s] = acc_r[n_col - s].astype(bf16)
                row_sum(n_col - s, True, True)

        @pl.when(c == n_col - 1)
        def _():
            @pl.loop(0, n_col - 1)
            def _(d):
                row_send[d] = acc_r[d].astype(bf16)
                row_sum(d, False, True)

    def reduce_rows(t):
        def one(d, up, ahead, landing, recv_sem):
            @pl.when(ahead)
            def _():
                arrived(landing.at[d], recv_sem.at[d])
                row_send[d] = (acc_r[d] + landing[d].astype(f32)).astype(bf16)
                row_sum(d, up, True)

        up = n_col - 1 - t + c
        down = t - (n_col - 1) + c
        one(up, True, both(0 < c, c < up, up < n_col), row_up, up_recv_sem)
        one(
            down, False, both(c < n_col - 1, c > down, down >= 0), row_down, down_recv_sem
        )

    gather_step(1)
    rows_step(0, True)
    to_cols(c, True)

    @pl.loop(1, max(chips, n_col - 2))
    def _(j):
        rows_step(j)

        @pl.when(j < n_col - 2)
        def _():
            gather_step(j + 1)

    start_rows()

    @pl.loop(1, n_col - 1)
    def _(s):
        cols_step(s)

    if n_col > 2:
        gather_step(n_col - 1)
    cols_step(n_col - 1)

    here = pl.ds(pl.multiple_of(q * rows, rows), rows)
    there = pl.ds(pl.multiple_of(other * rows, rows), rows)

    @pl.loop(0, k + 1)
    def _(kk):
        sib_send[kk] = acc_c[kk, :, there].astype(bf16)
        pair(kk, True)

    reduce_rows(1)

    @pl.loop(0, k)
    def _(kk):
        arrived(sib_recv.at[kk], pair_recv_sem.at[kk])
        col_send[kk] = (acc_c[kk, :, here] + sib_recv[kk].astype(f32)).astype(bf16)
        col_sum(kk).start()

    @pl.loop(2, n_col - 1)
    def _(t):
        reduce_rows(t)

    in_copy.wait()
    out_copy.wait()

    @pl.when(q == 0)
    def _():
        arrived(sib_recv.at[k], pair_recv_sem.at[k])
        acc_c[k, :, here] += sib_recv[k].astype(f32)

    @pl.when(c > 0)
    def _():
        arrived(row_up.at[c], up_recv_sem.at[c])
        acc_r[c] += row_up[c].astype(f32)

    @pl.when(c < n_col - 1)
    def _():
        arrived(row_down.at[c], down_recv_sem.at[c])
        acc_r[c] += row_down[c].astype(f32)

    @pl.loop(k + 1, chips)
    def _(kk):
        arrived(col_recv.at[kk], col_recv_sem.at[kk])
        acc_c[k, :, here] += col_recv[kk].astype(f32)

    combined = (x_ref[...].astype(f32) + acc_r[c] + acc_c[k, :, here].T).astype(bf16)
    hid = w_in.shape[1]
    part = min(hid, 256)
    total = jnp.zeros(out_ref.shape, f32) + bias_out_ref[...]
    for j in range(0, hid, part):
        hidden = jnp.dot(combined, w_in[:, j : j + part], preferred_element_type=f32)
        hidden = jnp.maximum(hidden + bias_in_ref[:, j : j + part], 0.0)
        total += jnp.dot(
            hidden.astype(bf16), w_out[j : j + part, :], preferred_element_type=f32
        )
    out_ref[...] = total.astype(bf16)

    gather_up(c, False)
    gather_down(c, False)
    to_sibling(k, False)
    for kk in range(1, chips):
        plane(kk, False)

    @pl.loop(1, n_col)
    def _(s):
        gather_up(c - s, False)
        gather_down(c + s, False)
        row_sum(n_col - s, True, False)
        row_sum(s - 1, False, False)

    @pl.loop(0, k)
    def _(kk):
        to_sibling(kk, False)
        pair(kk, False)
        col_sum(kk).wait_send()

    pair(k, False)


def solution(mesh):
    n_row = mesh.shape["row"]
    n_col = mesh.shape["col"]
    chips = n_row // CORES

    def shards(
        features, adjacency, tile_row, tile_column, tile_count, weight_in, bias_in, weight_out, bias_out
    ):
        rows, width = features.shape
        cap = adjacency.shape[1]
        blocks = rows // TILE
        places = n_row * n_col * blocks * blocks
        bf16, f32 = jnp.bfloat16, jnp.float32
        dma = pltpu.SemaphoreType.DMA
        vmem = pl.BlockSpec(memory_space=pltpu.VMEM)
        anywhere = pl.BlockSpec(memory_space=pl.ANY)
        scratch = [
            pltpu.VMEM((cap + 1, TILE, TILE), bf16),
            pltpu.VMEM((chips, n_col * rows, CORES * rows), bf16),
            pltpu.VMEM((8, -(-cap // TILE) * TILE), jnp.int32),
            pltpu.VMEM((1, places), jnp.int32),
            pltpu.SMEM((1, places), jnp.int32),
            pltpu.VMEM(weight_in.shape, bf16),
            pltpu.VMEM(weight_out.shape, bf16),
            pltpu.VMEM((chips, CORES * rows, width), bf16),
            pltpu.VMEM((n_col, width, rows), bf16),
            pltpu.VMEM((n_col, rows, width), f32),
            pltpu.VMEM((chips, width, CORES * rows), f32),
            pltpu.VMEM((n_col, rows, width), bf16),
            pltpu.VMEM((n_col, rows, width), bf16),
            pltpu.VMEM((n_col, rows, width), bf16),
            pltpu.VMEM((chips, width, rows), bf16),
            pltpu.VMEM((chips, width, rows), bf16),
            pltpu.VMEM((chips, width, rows), bf16),
            pltpu.VMEM((chips, width, rows), bf16),
            dma((4,)),
            dma((n_col,)),
            dma((n_col,)),
            dma((n_col,)),
            dma((chips,)),
            dma((n_row,)),
            dma((chips,)),
            dma((n_col,)),
            dma((n_col,)),
            dma((n_col,)),
            dma((n_col,)),
            dma((chips,)),
            dma((chips,)),
            dma((chips,)),
            dma((chips,)),
        ]
        return pl.pallas_call(
            functools.partial(kernel, n_row, n_col),
            out_shape=jax.ShapeDtypeStruct((rows, width), bf16),
            in_specs=[
                vmem,
                anywhere,
                vmem,
                vmem,
                pl.BlockSpec(memory_space=pltpu.SMEM),
                anywhere,
                vmem,
                anywhere,
                vmem,
            ],
            out_specs=vmem,
            scratch_shapes=scratch,
            compiler_params=pltpu.CompilerParams(
                collective_id=0, has_side_effects=True, vmem_limit_bytes=56 * 1024 * 1024
            ),
            name="gin_layer",
        )(
            features,
            adjacency,
            tile_row,
            tile_column,
            tile_count,
            weight_in,
            bias_in.reshape(1, -1),
            weight_out,
            bias_out.reshape(1, -1),
        )

    placed = (
        P(("row", "col"), None),
        P(("row", "col"), None, None, None),
        P(("row", "col"), None),
        P(("row", "col"), None),
        P(("row", "col")),
        P(),
        P(),
        P(),
        P(),
    )
    return jax.shard_map(
        shards, mesh=mesh, in_specs=placed, out_specs=P(("row", "col"), None), check_vma=False
    )
```

```python
import functools

import jax
import jax.numpy as jnp
from jax import lax
from jax.experimental import pallas as pl
from jax.experimental.pallas import tpu as pltpu
from jax.sharding import PartitionSpec as P

TILE = 128
CORES = 2
MESH = pl.DeviceIdType.MESH


def both(*conditions):
    result = conditions[0]
    for condition in conditions[1:]:
        result = jnp.logical_and(result, condition)
    return result


def kernel(
    n_row,
    n_col,
    x_ref,
    adjacency_ref,
    tile_row_ref,
    tile_column_ref,
    count_ref,
    weight_in_ref,
    bias_in_ref,
    weight_out_ref,
    bias_out_ref,
    out_ref,
    adj,
    dense,
    keys,
    slots_v,
    slots,
    w_in,
    w_out,
    xcol,
    xrow,
    acc_r,
    acc_c,
    row_send,
    row_up,
    row_down,
    sib_send,
    sib_recv,
    col_send,
    col_recv,
    local_sem,
    gather_up_sem,
    gather_down_sem,
    gather_recv_sem,
    plane_send_sem,
    plane_recv_sem,
    sibling_send_sem,
    up_send_sem,
    up_recv_sem,
    down_send_sem,
    down_recv_sem,
    pair_send_sem,
    pair_recv_sem,
    col_send_sem,
    col_recv_sem,
):
    _, width, rows = xrow.shape
    blocks = rows // TILE
    cap = adjacency_ref.shape[1]
    row_blocks = n_col * blocks
    col_blocks = n_row * blocks
    places = row_blocks * col_blocks
    chips = n_row // CORES
    wide = CORES * rows
    r = lax.axis_index("row")
    c = lax.axis_index("col")
    k = r // CORES
    q = r % CORES
    other = 1 - q
    sibling = (k * CORES + other, c)
    above = (r, c + 1)
    below = (r, c - 1)
    f32, bf16 = jnp.float32, jnp.bfloat16

    def remote(src, dst, send_sem, recv_sem, device):
        return pltpu.make_async_remote_copy(
            src_ref=src,
            dst_ref=dst,
            send_sem=send_sem,
            recv_sem=recv_sem,
            device_id=device,
            device_id_type=MESH,
        )

    def arrived(dst, sem):
        pltpu.make_async_copy(dst, dst, sem).wait()

    def run(condition, make, start):
        @pl.when(condition)
        def _():
            if start:
                make().start()
            else:
                make().wait_send()

    def gather_copy(b, up):
        sem = gather_up_sem if up else gather_down_sem
        device = above if up else below
        return remote(xrow.at[b], xrow.at[b], sem.at[b], gather_recv_sem.at[b], device)

    def gather_up(b, start):
        run(both(b >= 0, c < n_col - 1), lambda: gather_copy(b, True), start)

    def gather_down(b, start):
        run(both(b < n_col, c > 0), lambda: gather_copy(b, False), start)

    def plane(kk, start):
        run(
            kk > k,
            lambda: remote(
                xcol.at[k, pl.ds(q * rows, rows)],
                xcol.at[k, pl.ds(q * rows, rows)],
                plane_send_sem.at[kk],
                plane_recv_sem.at[r],
                (kk * CORES + q, c),
            ),
            start,
        )

    def to_sibling(kk, start):
        run(
            jnp.logical_or(kk < k, q == 0),
            lambda: remote(
                xcol.at[kk, pl.ds(q * rows, rows)],
                xcol.at[kk, pl.ds(q * rows, rows)],
                sibling_send_sem.at[kk],
                plane_recv_sem.at[kk * CORES + q],
                sibling,
            ),
            start,
        )

    def row_sum(d, up, start):
        run(
            both(c < d, d < n_col) if up else both(c > d, d >= 0),
            lambda: remote(
                row_send.at[d],
                (row_up if up else row_down).at[d],
                (up_send_sem if up else down_send_sem).at[d],
                (up_recv_sem if up else down_recv_sem).at[d],
                above if up else below,
            ),
            start,
        )

    def pair(kk, start):
        run(
            jnp.logical_or(kk < k, q == 1),
            lambda: remote(
                sib_send.at[kk],
                sib_recv.at[kk],
                pair_send_sem.at[kk],
                pair_recv_sem.at[kk],
                sibling,
            ),
            start,
        )

    def col_sum(kk):
        return remote(
            col_send.at[kk],
            col_recv.at[k],
            col_send_sem.at[kk],
            col_recv_sem.at[k],
            (kk * CORES + q, c),
        )

    barrier = pltpu.get_barrier_semaphore()
    pl.semaphore_signal(barrier, inc=1, device_id=sibling, device_id_type=MESH)
    for kk in range(chips):

        @pl.when(k != kk)
        def _():
            pl.semaphore_signal(
                barrier, inc=1, device_id=(kk * CORES + q, c), device_id_type=MESH
            )

    @pl.when(c > 0)
    def _():
        pl.semaphore_signal(barrier, inc=1, device_id=below, device_id_type=MESH)

    @pl.when(c < n_col - 1)
    def _():
        pl.semaphore_signal(barrier, inc=1, device_id=above, device_id_type=MESH)

    adj_copy = pltpu.make_async_copy(
        adjacency_ref.at[0], adj.at[pl.ds(0, cap)], local_sem.at[0]
    )
    adj_copy.start()
    in_copy = pltpu.make_async_copy(weight_in_ref, w_in, local_sem.at[1])
    in_copy.start()
    out_copy = pltpu.make_async_copy(weight_out_ref, w_out, local_sem.at[2])
    out_copy.start()

    xcol[k, pl.ds(pl.multiple_of(q * rows, rows), rows)] = x_ref[...]
    xrow[c] = x_ref[...].T

    has_below = (c + n_col - 1) // n_col
    has_above = (2 * n_col - 2 - c) // n_col
    pl.semaphore_wait(barrier, chips + has_below + has_above)

    gather_up(c, True)
    gather_down(c, True)
    to_sibling(k, True)
    for kk in range(1, chips):
        plane(kk, True)

    @pl.when(q == 0)
    def _():
        xcol[k, pl.ds(rows, rows)] = jnp.zeros((rows, width), bf16)

    lanes = keys.shape[1]
    keys[...] = jnp.full(keys.shape, -1, jnp.int32)
    slot_row = lax.broadcasted_iota(jnp.int32, (1, cap), 1)
    keys[0:1, 0:cap] = jnp.where(
        slot_row < count_ref[0],
        tile_row_ref[...] * col_blocks + tile_column_ref[...],
        -1,
    )
    key_column = jnp.broadcast_to(keys[0:1, :], (TILE, lanes)).T[:, 0:1]
    hit = key_column == lax.broadcasted_iota(jnp.int32, (lanes, places), 1)
    number = lax.broadcasted_iota(jnp.int32, (lanes, places), 0)
    slots_v[...] = cap + jnp.sum(
        jnp.where(hit, number - cap, 0), axis=0, keepdims=True
    )
    slot_copy = pltpu.make_async_copy(slots_v, slots, local_sem.at[3])
    slot_copy.start()
    adj[cap] = jnp.zeros((TILE, TILE), bf16)

    slot_copy.wait()
    adj_copy.wait()

    @pl.loop(0, chips)
    def _(kk):
        for i in range(row_blocks):
            for b in range(CORES * blocks):
                place = i * col_blocks + kk * (CORES * blocks) + b
                dense[kk, pl.ds(i * TILE, TILE), pl.ds(b * TILE, TILE)] = adj[
                    slots[0, place]
                ]

    def to_cols(source, first=False):
        part = pl.ds(pl.multiple_of(source * rows, rows), rows)
        for kk in range(chips):
            added = jnp.dot(xrow[source], dense[kk, part, :], preferred_element_type=f32)
            acc_c[kk] = added if first else acc_c[kk] + added

    def rows_step(j, first=False):
        @pl.when(j <= k)
        def _():
            kk = k - j
            mine = xcol.at[kk, pl.ds(q * rows, rows)]
            theirs = xcol.at[kk, pl.ds(other * rows, rows)]

            @pl.when(j > 0)
            def _():
                arrived(mine, plane_recv_sem.at[kk * CORES + q])
                to_sibling(kk, True)

            @pl.when(jnp.logical_or(j > 0, q == 1))
            def _():
                arrived(theirs, plane_recv_sem.at[kk * CORES + other])

            added = jnp.dot(dense[kk], xcol[kk], preferred_element_type=f32)
            added = added.reshape(acc_r.shape)
            acc_r[...] = added if first else acc_r[...] + added

    def gather_step(s):
        low, high = c - s, c + s

        @pl.when(low >= 0)
        def _():
            arrived(xrow.at[low], gather_recv_sem.at[low])

        gather_up(low, True)

        @pl.when(high < n_col)
        def _():
            arrived(xrow.at[high], gather_recv_sem.at[high])

        gather_down(high, True)

    def cols_step(s):
        @pl.loop(0, 2)
        def _(u):
            source = c - s + 2 * s * u

            @pl.when(both(source >= 0, source < n_col))
            def _():
                to_cols(source)

    def start_rows(t):
        up = n_col - 1 - t

        @pl.when(c == 0)
        def _():
            row_send[up] = acc_r[up].astype(bf16)
            row_sum(up, True, True)

        @pl.when(c == n_col - 1)
        def _():
            row_send[t] = acc_r[t].astype(bf16)
            row_sum(t, False, True)

    def reduce_rows(t):
        def one(d, up, ahead, landing, recv_sem):
            @pl.when(ahead)
            def _():
                arrived(landing.at[d], recv_sem.at[d])
                row_send[d] = (acc_r[d] + landing[d].astype(f32)).astype(bf16)
                row_sum(d, up, True)

        up = n_col - 1 - t + c
        down = t - (n_col - 1) + c
        one(up, True, both(0 < c, c < up, up < n_col), row_up, up_recv_sem)
        one(
            down, False, both(c < n_col - 1, c > down, down >= 0), row_down, down_recv_sem
        )

    gather_step(1)
    rows_step(0, True)
    to_cols(c, True)

    @pl.loop(1, max(chips, n_col - 2))
    def _(j):
        rows_step(j)

        @pl.when(j < n_col - 2)
        def _():
            gather_step(j + 1)

    start_rows(0)

    @pl.loop(1, n_col - 1)
    def _(s):
        cols_step(s)

    if n_col > 2:
        start_rows(1)

    if n_col > 2:
        gather_step(n_col - 1)
    cols_step(n_col - 1)

    here = pl.ds(pl.multiple_of(q * rows, rows), rows)
    there = pl.ds(pl.multiple_of(other * rows, rows), rows)

    @pl.loop(0, k + 1)
    def _(kk):
        sib_send[kk] = acc_c[kk, :, there].astype(bf16)
        pair(kk, True)

    @pl.loop(2, n_col - 1)
    def _(t):
        start_rows(t)

    reduce_rows(1)

    @pl.loop(0, k)
    def _(kk):
        arrived(sib_recv.at[kk], pair_recv_sem.at[kk])
        col_send[kk] = (acc_c[kk, :, here] + sib_recv[kk].astype(f32)).astype(bf16)
        col_sum(kk).start()

    @pl.loop(2, n_col - 1)
    def _(t):
        reduce_rows(t)

    in_copy.wait()
    out_copy.wait()

    @pl.when(q == 0)
    def _():
        arrived(sib_recv.at[k], pair_recv_sem.at[k])
        acc_c[k, :, here] += sib_recv[k].astype(f32)

    @pl.when(c > 0)
    def _():
        arrived(row_up.at[c], up_recv_sem.at[c])
        acc_r[c] += row_up[c].astype(f32)

    @pl.when(c < n_col - 1)
    def _():
        arrived(row_down.at[c], down_recv_sem.at[c])
        acc_r[c] += row_down[c].astype(f32)

    @pl.loop(k + 1, chips)
    def _(kk):
        arrived(col_recv.at[kk], col_recv_sem.at[kk])
        acc_c[k, :, here] += col_recv[kk].astype(f32)

    combined = (x_ref[...].astype(f32) + acc_r[c] + acc_c[k, :, here].T).astype(bf16)
    hid = w_in.shape[1]
    part = min(hid, 256)
    total = jnp.zeros(out_ref.shape, f32) + bias_out_ref[...]
    for j in range(0, hid, part):
        hidden = jnp.dot(combined, w_in[:, j : j + part], preferred_element_type=f32)
        hidden = jnp.maximum(hidden + bias_in_ref[:, j : j + part], 0.0)
        total += jnp.dot(
            hidden.astype(bf16), w_out[j : j + part, :], preferred_element_type=f32
        )
    out_ref[...] = total.astype(bf16)

    gather_up(c, False)
    gather_down(c, False)
    to_sibling(k, False)
    for kk in range(1, chips):
        plane(kk, False)

    @pl.loop(1, n_col)
    def _(s):
        gather_up(c - s, False)
        gather_down(c + s, False)
        row_sum(n_col - s, True, False)
        row_sum(s - 1, False, False)

    @pl.loop(0, k)
    def _(kk):
        to_sibling(kk, False)
        pair(kk, False)
        col_sum(kk).wait_send()

    pair(k, False)


def solution(mesh):
    n_row = mesh.shape["row"]
    n_col = mesh.shape["col"]
    chips = n_row // CORES

    def shards(
        features, adjacency, tile_row, tile_column, tile_count, weight_in, bias_in, weight_out, bias_out
    ):
        rows, width = features.shape
        cap = adjacency.shape[1]
        blocks = rows // TILE
        places = n_row * n_col * blocks * blocks
        bf16, f32 = jnp.bfloat16, jnp.float32
        dma = pltpu.SemaphoreType.DMA
        vmem = pl.BlockSpec(memory_space=pltpu.VMEM)
        anywhere = pl.BlockSpec(memory_space=pl.ANY)
        scratch = [
            pltpu.VMEM((cap + 1, TILE, TILE), bf16),
            pltpu.VMEM((chips, n_col * rows, CORES * rows), bf16),
            pltpu.VMEM((8, -(-cap // TILE) * TILE), jnp.int32),
            pltpu.VMEM((1, places), jnp.int32),
            pltpu.SMEM((1, places), jnp.int32),
            pltpu.VMEM(weight_in.shape, bf16),
            pltpu.VMEM(weight_out.shape, bf16),
            pltpu.VMEM((chips, CORES * rows, width), bf16),
            pltpu.VMEM((n_col, width, rows), bf16),
            pltpu.VMEM((n_col, rows, width), f32),
            pltpu.VMEM((chips, width, CORES * rows), f32),
            pltpu.VMEM((n_col, rows, width), bf16),
            pltpu.VMEM((n_col, rows, width), bf16),
            pltpu.VMEM((n_col, rows, width), bf16),
            pltpu.VMEM((chips, width, rows), bf16),
            pltpu.VMEM((chips, width, rows), bf16),
            pltpu.VMEM((chips, width, rows), bf16),
            pltpu.VMEM((chips, width, rows), bf16),
            dma((4,)),
            dma((n_col,)),
            dma((n_col,)),
            dma((n_col,)),
            dma((chips,)),
            dma((n_row,)),
            dma((chips,)),
            dma((n_col,)),
            dma((n_col,)),
            dma((n_col,)),
            dma((n_col,)),
            dma((chips,)),
            dma((chips,)),
            dma((chips,)),
            dma((chips,)),
        ]
        return pl.pallas_call(
            functools.partial(kernel, n_row, n_col),
            out_shape=jax.ShapeDtypeStruct((rows, width), bf16),
            in_specs=[
                vmem,
                anywhere,
                vmem,
                vmem,
                pl.BlockSpec(memory_space=pltpu.SMEM),
                anywhere,
                vmem,
                anywhere,
                vmem,
            ],
            out_specs=vmem,
            scratch_shapes=scratch,
            compiler_params=pltpu.CompilerParams(
                collective_id=0, has_side_effects=True, vmem_limit_bytes=56 * 1024 * 1024
            ),
            name="gin_layer",
        )(
            features,
            adjacency,
            tile_row,
            tile_column,
            tile_count,
            weight_in,
            bias_in.reshape(1, -1),
            weight_out,
            bias_out.reshape(1, -1),
        )

    placed = (
        P(("row", "col"), None),
        P(("row", "col"), None, None, None),
        P(("row", "col"), None),
        P(("row", "col"), None),
        P(("row", "col")),
        P(),
        P(),
        P(),
        P(),
    )
    return jax.shard_map(
        shards, mesh=mesh, in_specs=placed, out_specs=P(("row", "col"), None), check_vma=False
    )
```

```python
import functools

import jax
import jax.numpy as jnp
from jax import lax
from jax.experimental import pallas as pl
from jax.experimental.pallas import tpu as pltpu
from jax.sharding import PartitionSpec as P

TILE = 128
CORES = 2
PIECES = 2
MESH = pl.DeviceIdType.MESH


def both(*conditions):
    result = conditions[0]
    for condition in conditions[1:]:
        result = jnp.logical_and(result, condition)
    return result


def kernel(
    n_row,
    n_col,
    x_ref,
    adjacency_ref,
    tile_row_ref,
    tile_column_ref,
    count_ref,
    weight_in_ref,
    bias_in_ref,
    weight_out_ref,
    bias_out_ref,
    out_ref,
    adj,
    dense,
    keys,
    slots_v,
    slots,
    w_in,
    w_out,
    xcol,
    xrow,
    acc_r,
    acc_c,
    row_send,
    row_up,
    row_down,
    sib_send,
    sib_recv,
    col_send,
    col_recv,
    local_sem,
    gather_up_sem,
    gather_down_sem,
    gather_recv_sem,
    plane_send_sem,
    plane_recv_sem,
    sibling_send_sem,
    up_send_sem,
    up_recv_sem,
    down_send_sem,
    down_recv_sem,
    pair_send_sem,
    pair_recv_sem,
    col_send_sem,
    col_recv_sem,
):
    _, width, rows = xrow.shape
    blocks = rows // TILE
    cap = adjacency_ref.shape[1]
    row_blocks = n_col * blocks
    col_blocks = n_row * blocks
    places = row_blocks * col_blocks
    chips = n_row // CORES
    wide = CORES * rows
    r = lax.axis_index("row")
    c = lax.axis_index("col")
    k = r // CORES
    q = r % CORES
    other = 1 - q
    sibling = (k * CORES + other, c)
    above = (r, c + 1)
    below = (r, c - 1)
    f32, bf16 = jnp.float32, jnp.bfloat16

    def remote(src, dst, send_sem, recv_sem, device):
        return pltpu.make_async_remote_copy(
            src_ref=src,
            dst_ref=dst,
            send_sem=send_sem,
            recv_sem=recv_sem,
            device_id=device,
            device_id_type=MESH,
        )

    def arrived(dst, sem):
        pltpu.make_async_copy(dst, dst, sem).wait()

    def run(condition, make, start):
        @pl.when(condition)
        def _():
            if start:
                make().start()
            else:
                make().wait_send()

    def gather_copy(b, up):
        sem = gather_up_sem if up else gather_down_sem
        device = above if up else below
        return remote(xrow.at[b], xrow.at[b], sem.at[b], gather_recv_sem.at[b], device)

    def gather_up(b, start):
        run(both(b >= 0, c < n_col - 1), lambda: gather_copy(b, True), start)

    def gather_down(b, start):
        run(both(b < n_col, c > 0), lambda: gather_copy(b, False), start)

    def plane(kk, start):
        run(
            kk > k,
            lambda: remote(
                xcol.at[k, pl.ds(q * rows, rows)],
                xcol.at[k, pl.ds(q * rows, rows)],
                plane_send_sem.at[kk],
                plane_recv_sem.at[r],
                (kk * CORES + q, c),
            ),
            start,
        )

    def to_sibling(kk, start):
        run(
            jnp.logical_or(kk < k, q == 0),
            lambda: remote(
                xcol.at[kk, pl.ds(q * rows, rows)],
                xcol.at[kk, pl.ds(q * rows, rows)],
                sibling_send_sem.at[kk],
                plane_recv_sem.at[kk * CORES + q],
                sibling,
            ),
            start,
        )

    def piece(p):
        return pl.ds(p * (rows // PIECES), rows // PIECES)

    def row_sum(d, up, start):
        for p in range(PIECES):
            row_piece(d, p, up, start)

    def row_piece(d, p, up, start):
        run(
            both(c < d, d < n_col) if up else both(c > d, d >= 0),
            lambda: remote(
                row_send.at[d, piece(p)],
                (row_up if up else row_down).at[d, piece(p)],
                (up_send_sem if up else down_send_sem).at[p, d],
                (up_recv_sem if up else down_recv_sem).at[p, d],
                above if up else below,
            ),
            start,
        )

    def pair(kk, start):
        run(
            jnp.logical_or(kk < k, q == 1),
            lambda: remote(
                sib_send.at[kk],
                sib_recv.at[kk],
                pair_send_sem.at[kk],
                pair_recv_sem.at[kk],
                sibling,
            ),
            start,
        )

    def col_sum(kk):
        return remote(
            col_send.at[kk],
            col_recv.at[k],
            col_send_sem.at[kk],
            col_recv_sem.at[k],
            (kk * CORES + q, c),
        )

    barrier = pltpu.get_barrier_semaphore()
    pl.semaphore_signal(barrier, inc=1, device_id=sibling, device_id_type=MESH)
    for kk in range(chips):

        @pl.when(k != kk)
        def _():
            pl.semaphore_signal(
                barrier, inc=1, device_id=(kk * CORES + q, c), device_id_type=MESH
            )

    @pl.when(c > 0)
    def _():
        pl.semaphore_signal(barrier, inc=1, device_id=below, device_id_type=MESH)

    @pl.when(c < n_col - 1)
    def _():
        pl.semaphore_signal(barrier, inc=1, device_id=above, device_id_type=MESH)

    adj_copy = pltpu.make_async_copy(
        adjacency_ref.at[0], adj.at[pl.ds(0, cap)], local_sem.at[0]
    )
    adj_copy.start()
    in_copy = pltpu.make_async_copy(weight_in_ref, w_in, local_sem.at[1])
    in_copy.start()
    out_copy = pltpu.make_async_copy(weight_out_ref, w_out, local_sem.at[2])
    out_copy.start()

    xcol[k, pl.ds(pl.multiple_of(q * rows, rows), rows)] = x_ref[...]
    xrow[c] = x_ref[...].T

    has_below = (c + n_col - 1) // n_col
    has_above = (2 * n_col - 2 - c) // n_col
    pl.semaphore_wait(barrier, chips + has_below + has_above)

    gather_up(c, True)
    gather_down(c, True)
    to_sibling(k, True)
    for kk in range(1, chips):
        plane(kk, True)

    @pl.when(q == 0)
    def _():
        xcol[k, pl.ds(rows, rows)] = jnp.zeros((rows, width), bf16)

    lanes = keys.shape[1]
    keys[...] = jnp.full(keys.shape, -1, jnp.int32)
    slot_row = lax.broadcasted_iota(jnp.int32, (1, cap), 1)
    keys[0:1, 0:cap] = jnp.where(
        slot_row < count_ref[0],
        tile_row_ref[...] * col_blocks + tile_column_ref[...],
        -1,
    )
    key_column = jnp.broadcast_to(keys[0:1, :], (TILE, lanes)).T[:, 0:1]
    hit = key_column == lax.broadcasted_iota(jnp.int32, (lanes, places), 1)
    number = lax.broadcasted_iota(jnp.int32, (lanes, places), 0)
    slots_v[...] = cap + jnp.sum(
        jnp.where(hit, number - cap, 0), axis=0, keepdims=True
    )
    slot_copy = pltpu.make_async_copy(slots_v, slots, local_sem.at[3])
    slot_copy.start()
    adj[cap] = jnp.zeros((TILE, TILE), bf16)

    slot_copy.wait()
    adj_copy.wait()

    @pl.loop(0, chips)
    def _(kk):
        for i in range(row_blocks):
            for b in range(CORES * blocks):
                place = i * col_blocks + kk * (CORES * blocks) + b
                dense[kk, pl.ds(i * TILE, TILE), pl.ds(b * TILE, TILE)] = adj[
                    slots[0, place]
                ]

    def to_cols(source, first=False):
        part = pl.ds(pl.multiple_of(source * rows, rows), rows)
        for kk in range(chips):
            added = jnp.dot(xrow[source], dense[kk, part, :], preferred_element_type=f32)
            acc_c[kk] = added if first else acc_c[kk] + added

    def rows_step(j, first=False):
        @pl.when(j <= k)
        def _():
            kk = k - j
            mine = xcol.at[kk, pl.ds(q * rows, rows)]
            theirs = xcol.at[kk, pl.ds(other * rows, rows)]

            @pl.when(j > 0)
            def _():
                arrived(mine, plane_recv_sem.at[kk * CORES + q])
                to_sibling(kk, True)

            @pl.when(jnp.logical_or(j > 0, q == 1))
            def _():
                arrived(theirs, plane_recv_sem.at[kk * CORES + other])

            added = jnp.dot(dense[kk], xcol[kk], preferred_element_type=f32)
            added = added.reshape(acc_r.shape)
            acc_r[...] = added if first else acc_r[...] + added

    def gather_step(s):
        low, high = c - s, c + s

        @pl.when(low >= 0)
        def _():
            arrived(xrow.at[low], gather_recv_sem.at[low])

        gather_up(low, True)

        @pl.when(high < n_col)
        def _():
            arrived(xrow.at[high], gather_recv_sem.at[high])

        gather_down(high, True)

    def cols_step(s):
        @pl.loop(0, 2)
        def _(u):
            source = c - s + 2 * s * u

            @pl.when(both(source >= 0, source < n_col))
            def _():
                to_cols(source)

    def start_rows(t):
        up = n_col - 1 - t

        @pl.when(c == 0)
        def _():
            row_send[up] = acc_r[up].astype(bf16)
            row_sum(up, True, True)

        @pl.when(c == n_col - 1)
        def _():
            row_send[t] = acc_r[t].astype(bf16)
            row_sum(t, False, True)

    def reduce_rows(t):
        def one(d, p, up, ahead, landing, recv_sem):
            @pl.when(ahead)
            def _():
                part = piece(p)
                arrived(landing.at[d, part], recv_sem.at[p, d])
                row_send[d, part] = (
                    acc_r[d, part] + landing[d, part].astype(f32)
                ).astype(bf16)
                row_piece(d, p, up, True)

        up = n_col - 1 - t + c
        down = t - (n_col - 1) + c
        ahead_up = both(0 < c, c < up, up < n_col)
        ahead_down = both(c < n_col - 1, c > down, down >= 0)
        for p in range(PIECES):
            one(up, p, True, ahead_up, row_up, up_recv_sem)
            one(down, p, False, ahead_down, row_down, down_recv_sem)

    gather_step(1)
    rows_step(0, True)
    to_cols(c, True)

    @pl.loop(1, max(chips, n_col - 2))
    def _(j):
        rows_step(j)

        @pl.when(j < n_col - 2)
        def _():
            gather_step(j + 1)

    start_rows(0)

    @pl.loop(1, n_col - 1)
    def _(s):
        cols_step(s)

    if n_col > 2:
        start_rows(1)

    if n_col > 2:
        gather_step(n_col - 1)
    cols_step(n_col - 1)

    here = pl.ds(pl.multiple_of(q * rows, rows), rows)
    there = pl.ds(pl.multiple_of(other * rows, rows), rows)

    @pl.loop(0, k + 1)
    def _(kk):
        sib_send[kk] = acc_c[kk, :, there].astype(bf16)
        pair(kk, True)

    @pl.loop(2, n_col - 1)
    def _(t):
        start_rows(t)

    reduce_rows(1)

    @pl.loop(0, k)
    def _(kk):
        arrived(sib_recv.at[kk], pair_recv_sem.at[kk])
        col_send[kk] = (acc_c[kk, :, here] + sib_recv[kk].astype(f32)).astype(bf16)
        col_sum(kk).start()

    @pl.loop(2, n_col - 1)
    def _(t):
        reduce_rows(t)

    in_copy.wait()
    out_copy.wait()

    @pl.when(q == 0)
    def _():
        arrived(sib_recv.at[k], pair_recv_sem.at[k])
        acc_c[k, :, here] += sib_recv[k].astype(f32)

    @pl.loop(k + 1, chips)
    def _(kk):
        arrived(col_recv.at[kk], col_recv_sem.at[kk])
        acc_c[k, :, here] += col_recv[kk].astype(f32)

    acc_r[c] += x_ref[...].astype(f32) + acc_c[k, :, here].T
    for p in range(PIECES):
        part = piece(p)

        @pl.when(c > 0)
        def _():
            arrived(row_up.at[c, part], up_recv_sem.at[p, c])
            acc_r[c, part] += row_up[c, part].astype(f32)

        @pl.when(c < n_col - 1)
        def _():
            arrived(row_down.at[c, part], down_recv_sem.at[p, c])
            acc_r[c, part] += row_down[c, part].astype(f32)

    combined = acc_r[c].astype(bf16)
    hid = w_in.shape[1]
    part = min(hid, 256)
    total = jnp.zeros(out_ref.shape, f32) + bias_out_ref[...]
    for j in range(0, hid, part):
        hidden = jnp.dot(combined, w_in[:, j : j + part], preferred_element_type=f32)
        hidden = jnp.maximum(hidden + bias_in_ref[:, j : j + part], 0.0)
        total += jnp.dot(
            hidden.astype(bf16), w_out[j : j + part, :], preferred_element_type=f32
        )
    out_ref[...] = total.astype(bf16)

    gather_up(c, False)
    gather_down(c, False)
    to_sibling(k, False)
    for kk in range(1, chips):
        plane(kk, False)

    @pl.loop(1, n_col)
    def _(s):
        gather_up(c - s, False)
        gather_down(c + s, False)
        row_sum(n_col - s, True, False)
        row_sum(s - 1, False, False)

    @pl.loop(0, k)
    def _(kk):
        to_sibling(kk, False)
        pair(kk, False)
        col_sum(kk).wait_send()

    pair(k, False)


def solution(mesh):
    n_row = mesh.shape["row"]
    n_col = mesh.shape["col"]
    chips = n_row // CORES

    def shards(
        features, adjacency, tile_row, tile_column, tile_count, weight_in, bias_in, weight_out, bias_out
    ):
        rows, width = features.shape
        cap = adjacency.shape[1]
        blocks = rows // TILE
        places = n_row * n_col * blocks * blocks
        bf16, f32 = jnp.bfloat16, jnp.float32
        dma = pltpu.SemaphoreType.DMA
        vmem = pl.BlockSpec(memory_space=pltpu.VMEM)
        anywhere = pl.BlockSpec(memory_space=pl.ANY)
        scratch = [
            pltpu.VMEM((cap + 1, TILE, TILE), bf16),
            pltpu.VMEM((chips, n_col * rows, CORES * rows), bf16),
            pltpu.VMEM((8, -(-cap // TILE) * TILE), jnp.int32),
            pltpu.VMEM((1, places), jnp.int32),
            pltpu.SMEM((1, places), jnp.int32),
            pltpu.VMEM(weight_in.shape, bf16),
            pltpu.VMEM(weight_out.shape, bf16),
            pltpu.VMEM((chips, CORES * rows, width), bf16),
            pltpu.VMEM((n_col, width, rows), bf16),
            pltpu.VMEM((n_col, rows, width), f32),
            pltpu.VMEM((chips, width, CORES * rows), f32),
            pltpu.VMEM((n_col, rows, width), bf16),
            pltpu.VMEM((n_col, rows, width), bf16),
            pltpu.VMEM((n_col, rows, width), bf16),
            pltpu.VMEM((chips, width, rows), bf16),
            pltpu.VMEM((chips, width, rows), bf16),
            pltpu.VMEM((chips, width, rows), bf16),
            pltpu.VMEM((chips, width, rows), bf16),
            dma((4,)),
            dma((n_col,)),
            dma((n_col,)),
            dma((n_col,)),
            dma((chips,)),
            dma((n_row,)),
            dma((chips,)),
            dma((PIECES, n_col)),
            dma((PIECES, n_col)),
            dma((PIECES, n_col)),
            dma((PIECES, n_col)),
            dma((chips,)),
            dma((chips,)),
            dma((chips,)),
            dma((chips,)),
        ]
        return pl.pallas_call(
            functools.partial(kernel, n_row, n_col),
            out_shape=jax.ShapeDtypeStruct((rows, width), bf16),
            in_specs=[
                vmem,
                anywhere,
                vmem,
                vmem,
                pl.BlockSpec(memory_space=pltpu.SMEM),
                anywhere,
                vmem,
                anywhere,
                vmem,
            ],
            out_specs=vmem,
            scratch_shapes=scratch,
            compiler_params=pltpu.CompilerParams(
                collective_id=0, has_side_effects=True, vmem_limit_bytes=56 * 1024 * 1024
            ),
            name="gin_layer",
        )(
            features,
            adjacency,
            tile_row,
            tile_column,
            tile_count,
            weight_in,
            bias_in.reshape(1, -1),
            weight_out,
            bias_out.reshape(1, -1),
        )

    placed = (
        P(("row", "col"), None),
        P(("row", "col"), None, None, None),
        P(("row", "col"), None),
        P(("row", "col"), None),
        P(("row", "col")),
        P(),
        P(),
        P(),
        P(),
    )
    return jax.shard_map(
        shards, mesh=mesh, in_specs=placed, out_specs=P(("row", "col"), None), check_vma=False
    )
```

```python
import functools

import jax
import jax.numpy as jnp
from jax import lax
from jax.experimental import pallas as pl
from jax.experimental.pallas import tpu as pltpu
from jax.sharding import PartitionSpec as P

TILE = 128
CORES = 2
PIECES = 4
MESH = pl.DeviceIdType.MESH


def both(*conditions):
    result = conditions[0]
    for condition in conditions[1:]:
        result = jnp.logical_and(result, condition)
    return result


def kernel(
    n_row,
    n_col,
    x_ref,
    adjacency_ref,
    tile_row_ref,
    tile_column_ref,
    count_ref,
    weight_in_ref,
    bias_in_ref,
    weight_out_ref,
    bias_out_ref,
    out_ref,
    adj,
    dense,
    keys,
    slots_v,
    slots,
    w_in,
    w_out,
    xcol,
    xrow,
    acc_r,
    acc_c,
    row_send,
    row_up,
    row_down,
    sib_send,
    sib_recv,
    col_send,
    col_recv,
    local_sem,
    gather_up_sem,
    gather_down_sem,
    gather_recv_sem,
    plane_send_sem,
    plane_recv_sem,
    sibling_send_sem,
    up_send_sem,
    up_recv_sem,
    down_send_sem,
    down_recv_sem,
    pair_send_sem,
    pair_recv_sem,
    col_send_sem,
    col_recv_sem,
):
    _, width, rows = xrow.shape
    blocks = rows // TILE
    cap = adjacency_ref.shape[1]
    row_blocks = n_col * blocks
    col_blocks = n_row * blocks
    places = row_blocks * col_blocks
    chips = n_row // CORES
    wide = CORES * rows
    r = lax.axis_index("row")
    c = lax.axis_index("col")
    k = r // CORES
    q = r % CORES
    other = 1 - q
    sibling = (k * CORES + other, c)
    above = (r, c + 1)
    below = (r, c - 1)
    f32, bf16 = jnp.float32, jnp.bfloat16

    def remote(src, dst, send_sem, recv_sem, device):
        return pltpu.make_async_remote_copy(
            src_ref=src,
            dst_ref=dst,
            send_sem=send_sem,
            recv_sem=recv_sem,
            device_id=device,
            device_id_type=MESH,
        )

    def arrived(dst, sem):
        pltpu.make_async_copy(dst, dst, sem).wait()

    def run(condition, make, start):
        @pl.when(condition)
        def _():
            if start:
                make().start()
            else:
                make().wait_send()

    def gather_copy(b, up):
        sem = gather_up_sem if up else gather_down_sem
        device = above if up else below
        return remote(xrow.at[b], xrow.at[b], sem.at[b], gather_recv_sem.at[b], device)

    def gather_up(b, start):
        run(both(b >= 0, c < n_col - 1), lambda: gather_copy(b, True), start)

    def gather_down(b, start):
        run(both(b < n_col, c > 0), lambda: gather_copy(b, False), start)

    def plane(kk, start):
        run(
            kk > k,
            lambda: remote(
                xcol.at[k, pl.ds(q * rows, rows)],
                xcol.at[k, pl.ds(q * rows, rows)],
                plane_send_sem.at[kk],
                plane_recv_sem.at[r],
                (kk * CORES + q, c),
            ),
            start,
        )

    def to_sibling(kk, start):
        run(
            jnp.logical_or(kk < k, q == 0),
            lambda: remote(
                xcol.at[kk, pl.ds(q * rows, rows)],
                xcol.at[kk, pl.ds(q * rows, rows)],
                sibling_send_sem.at[kk],
                plane_recv_sem.at[kk * CORES + q],
                sibling,
            ),
            start,
        )

    def piece(p):
        return pl.ds(p * (rows // PIECES), rows // PIECES)

    def row_sum(d, up, start):
        for p in range(PIECES):
            row_piece(d, p, up, start)

    def row_piece(d, p, up, start):
        run(
            both(c < d, d < n_col) if up else both(c > d, d >= 0),
            lambda: remote(
                row_send.at[d, piece(p)],
                (row_up if up else row_down).at[d, piece(p)],
                (up_send_sem if up else down_send_sem).at[p, d],
                (up_recv_sem if up else down_recv_sem).at[p, d],
                above if up else below,
            ),
            start,
        )

    def pair(kk, start):
        run(
            jnp.logical_or(kk < k, q == 1),
            lambda: remote(
                sib_send.at[kk],
                sib_recv.at[kk],
                pair_send_sem.at[kk],
                pair_recv_sem.at[kk],
                sibling,
            ),
            start,
        )

    def col_sum(kk):
        return remote(
            col_send.at[kk],
            col_recv.at[k],
            col_send_sem.at[kk],
            col_recv_sem.at[k],
            (kk * CORES + q, c),
        )

    barrier = pltpu.get_barrier_semaphore()
    pl.semaphore_signal(barrier, inc=1, device_id=sibling, device_id_type=MESH)
    for kk in range(chips):

        @pl.when(k != kk)
        def _():
            pl.semaphore_signal(
                barrier, inc=1, device_id=(kk * CORES + q, c), device_id_type=MESH
            )

    @pl.when(c > 0)
    def _():
        pl.semaphore_signal(barrier, inc=1, device_id=below, device_id_type=MESH)

    @pl.when(c < n_col - 1)
    def _():
        pl.semaphore_signal(barrier, inc=1, device_id=above, device_id_type=MESH)

    adj_copy = pltpu.make_async_copy(
        adjacency_ref.at[0], adj.at[pl.ds(0, cap)], local_sem.at[0]
    )
    adj_copy.start()
    in_copy = pltpu.make_async_copy(weight_in_ref, w_in, local_sem.at[1])
    in_copy.start()
    out_copy = pltpu.make_async_copy(weight_out_ref, w_out, local_sem.at[2])
    out_copy.start()

    xcol[k, pl.ds(pl.multiple_of(q * rows, rows), rows)] = x_ref[...]
    xrow[c] = x_ref[...].T

    has_below = (c + n_col - 1) // n_col
    has_above = (2 * n_col - 2 - c) // n_col
    pl.semaphore_wait(barrier, chips + has_below + has_above)

    gather_up(c, True)
    gather_down(c, True)
    to_sibling(k, True)
    for kk in range(1, chips):
        plane(kk, True)

    @pl.when(q == 0)
    def _():
        xcol[k, pl.ds(rows, rows)] = jnp.zeros((rows, width), bf16)

    lanes = keys.shape[1]
    keys[...] = jnp.full(keys.shape, -1, jnp.int32)
    slot_row = lax.broadcasted_iota(jnp.int32, (1, cap), 1)
    keys[0:1, 0:cap] = jnp.where(
        slot_row < count_ref[0],
        tile_row_ref[...] * col_blocks + tile_column_ref[...],
        -1,
    )
    key_column = jnp.broadcast_to(keys[0:1, :], (TILE, lanes)).T[:, 0:1]
    hit = key_column == lax.broadcasted_iota(jnp.int32, (lanes, places), 1)
    number = lax.broadcasted_iota(jnp.int32, (lanes, places), 0)
    slots_v[...] = cap + jnp.sum(
        jnp.where(hit, number - cap, 0), axis=0, keepdims=True
    )
    slot_copy = pltpu.make_async_copy(slots_v, slots, local_sem.at[3])
    slot_copy.start()
    adj[cap] = jnp.zeros((TILE, TILE), bf16)

    slot_copy.wait()
    adj_copy.wait()

    @pl.loop(0, chips)
    def _(kk):
        for i in range(row_blocks):
            for b in range(CORES * blocks):
                place = i * col_blocks + kk * (CORES * blocks) + b
                dense[kk, pl.ds(i * TILE, TILE), pl.ds(b * TILE, TILE)] = adj[
                    slots[0, place]
                ]

    def to_cols(source, first=False):
        part = pl.ds(pl.multiple_of(source * rows, rows), rows)
        for kk in range(chips):
            added = jnp.dot(xrow[source], dense[kk, part, :], preferred_element_type=f32)
            acc_c[kk] = added if first else acc_c[kk] + added

    def rows_step(j, first=False):
        @pl.when(j <= k)
        def _():
            kk = k - j
            mine = xcol.at[kk, pl.ds(q * rows, rows)]
            theirs = xcol.at[kk, pl.ds(other * rows, rows)]

            @pl.when(j > 0)
            def _():
                arrived(mine, plane_recv_sem.at[kk * CORES + q])
                to_sibling(kk, True)

            @pl.when(jnp.logical_or(j > 0, q == 1))
            def _():
                arrived(theirs, plane_recv_sem.at[kk * CORES + other])

            added = jnp.dot(dense[kk], xcol[kk], preferred_element_type=f32)
            added = added.reshape(acc_r.shape)
            acc_r[...] = added if first else acc_r[...] + added

    def gather_step(s):
        low, high = c - s, c + s

        @pl.when(low >= 0)
        def _():
            arrived(xrow.at[low], gather_recv_sem.at[low])

        gather_up(low, True)

        @pl.when(high < n_col)
        def _():
            arrived(xrow.at[high], gather_recv_sem.at[high])

        gather_down(high, True)

    def cols_step(s):
        @pl.loop(0, 2)
        def _(u):
            source = c - s + 2 * s * u

            @pl.when(both(source >= 0, source < n_col))
            def _():
                to_cols(source)

    def start_rows(t):
        up = n_col - 1 - t

        @pl.when(c == 0)
        def _():
            row_send[up] = acc_r[up].astype(bf16)
            row_sum(up, True, True)

        @pl.when(c == n_col - 1)
        def _():
            row_send[t] = acc_r[t].astype(bf16)
            row_sum(t, False, True)

    def reduce_rows(t):
        def one(d, p, up, ahead, landing, recv_sem):
            @pl.when(ahead)
            def _():
                part = piece(p)
                arrived(landing.at[d, part], recv_sem.at[p, d])
                row_send[d, part] = (
                    acc_r[d, part] + landing[d, part].astype(f32)
                ).astype(bf16)
                row_piece(d, p, up, True)

        up = n_col - 1 - t + c
        down = t - (n_col - 1) + c
        ahead_up = both(0 < c, c < up, up < n_col)
        ahead_down = both(c < n_col - 1, c > down, down >= 0)
        for p in range(PIECES):
            one(up, p, True, ahead_up, row_up, up_recv_sem)
            one(down, p, False, ahead_down, row_down, down_recv_sem)

    gather_step(1)
    rows_step(0, True)
    to_cols(c, True)

    @pl.loop(1, max(chips, n_col - 2))
    def _(j):
        rows_step(j)

        @pl.when(j < n_col - 2)
        def _():
            gather_step(j + 1)

    start_rows(0)

    @pl.loop(1, n_col - 1)
    def _(s):
        cols_step(s)

    if n_col > 2:
        start_rows(1)

    if n_col > 2:
        gather_step(n_col - 1)
    cols_step(n_col - 1)

    here = pl.ds(pl.multiple_of(q * rows, rows), rows)
    there = pl.ds(pl.multiple_of(other * rows, rows), rows)

    @pl.loop(0, k + 1)
    def _(kk):
        sib_send[kk] = acc_c[kk, :, there].astype(bf16)
        pair(kk, True)

    @pl.loop(2, n_col - 1)
    def _(t):
        start_rows(t)

    reduce_rows(1)

    @pl.loop(0, k)
    def _(kk):
        arrived(sib_recv.at[kk], pair_recv_sem.at[kk])
        col_send[kk] = (acc_c[kk, :, here] + sib_recv[kk].astype(f32)).astype(bf16)
        col_sum(kk).start()

    @pl.loop(2, n_col - 1)
    def _(t):
        reduce_rows(t)

    in_copy.wait()
    out_copy.wait()

    @pl.when(q == 0)
    def _():
        arrived(sib_recv.at[k], pair_recv_sem.at[k])
        acc_c[k, :, here] += sib_recv[k].astype(f32)

    @pl.loop(k + 1, chips)
    def _(kk):
        arrived(col_recv.at[kk], col_recv_sem.at[kk])
        acc_c[k, :, here] += col_recv[kk].astype(f32)

    acc_r[c] += x_ref[...].astype(f32) + acc_c[k, :, here].T
    for p in range(PIECES):
        part = piece(p)

        @pl.when(c > 0)
        def _():
            arrived(row_up.at[c, part], up_recv_sem.at[p, c])
            acc_r[c, part] += row_up[c, part].astype(f32)

        @pl.when(c < n_col - 1)
        def _():
            arrived(row_down.at[c, part], down_recv_sem.at[p, c])
            acc_r[c, part] += row_down[c, part].astype(f32)

    combined = acc_r[c].astype(bf16)
    hid = w_in.shape[1]
    part = min(hid, 256)
    total = jnp.zeros(out_ref.shape, f32) + bias_out_ref[...]
    for j in range(0, hid, part):
        hidden = jnp.dot(combined, w_in[:, j : j + part], preferred_element_type=f32)
        hidden = jnp.maximum(hidden + bias_in_ref[:, j : j + part], 0.0)
        total += jnp.dot(
            hidden.astype(bf16), w_out[j : j + part, :], preferred_element_type=f32
        )
    out_ref[...] = total.astype(bf16)

    gather_up(c, False)
    gather_down(c, False)
    to_sibling(k, False)
    for kk in range(1, chips):
        plane(kk, False)

    @pl.loop(1, n_col)
    def _(s):
        gather_up(c - s, False)
        gather_down(c + s, False)
        row_sum(n_col - s, True, False)
        row_sum(s - 1, False, False)

    @pl.loop(0, k)
    def _(kk):
        to_sibling(kk, False)
        pair(kk, False)
        col_sum(kk).wait_send()

    pair(k, False)


def solution(mesh):
    n_row = mesh.shape["row"]
    n_col = mesh.shape["col"]
    chips = n_row // CORES

    def shards(
        features, adjacency, tile_row, tile_column, tile_count, weight_in, bias_in, weight_out, bias_out
    ):
        rows, width = features.shape
        cap = adjacency.shape[1]
        blocks = rows // TILE
        places = n_row * n_col * blocks * blocks
        bf16, f32 = jnp.bfloat16, jnp.float32
        dma = pltpu.SemaphoreType.DMA
        vmem = pl.BlockSpec(memory_space=pltpu.VMEM)
        anywhere = pl.BlockSpec(memory_space=pl.ANY)
        scratch = [
            pltpu.VMEM((cap + 1, TILE, TILE), bf16),
            pltpu.VMEM((chips, n_col * rows, CORES * rows), bf16),
            pltpu.VMEM((8, -(-cap // TILE) * TILE), jnp.int32),
            pltpu.VMEM((1, places), jnp.int32),
            pltpu.SMEM((1, places), jnp.int32),
            pltpu.VMEM(weight_in.shape, bf16),
            pltpu.VMEM(weight_out.shape, bf16),
            pltpu.VMEM((chips, CORES * rows, width), bf16),
            pltpu.VMEM((n_col, width, rows), bf16),
            pltpu.VMEM((n_col, rows, width), f32),
            pltpu.VMEM((chips, width, CORES * rows), f32),
            pltpu.VMEM((n_col, rows, width), bf16),
            pltpu.VMEM((n_col, rows, width), bf16),
            pltpu.VMEM((n_col, rows, width), bf16),
            pltpu.VMEM((chips, width, rows), bf16),
            pltpu.VMEM((chips, width, rows), bf16),
            pltpu.VMEM((chips, width, rows), bf16),
            pltpu.VMEM((chips, width, rows), bf16),
            dma((4,)),
            dma((n_col,)),
            dma((n_col,)),
            dma((n_col,)),
            dma((chips,)),
            dma((n_row,)),
            dma((chips,)),
            dma((PIECES, n_col)),
            dma((PIECES, n_col)),
            dma((PIECES, n_col)),
            dma((PIECES, n_col)),
            dma((chips,)),
            dma((chips,)),
            dma((chips,)),
            dma((chips,)),
        ]
        return pl.pallas_call(
            functools.partial(kernel, n_row, n_col),
            out_shape=jax.ShapeDtypeStruct((rows, width), bf16),
            in_specs=[
                vmem,
                anywhere,
                vmem,
                vmem,
                pl.BlockSpec(memory_space=pltpu.SMEM),
                anywhere,
                vmem,
                anywhere,
                vmem,
            ],
            out_specs=vmem,
            scratch_shapes=scratch,
            compiler_params=pltpu.CompilerParams(
                collective_id=0, has_side_effects=True, vmem_limit_bytes=56 * 1024 * 1024
            ),
            name="gin_layer",
        )(
            features,
            adjacency,
            tile_row,
            tile_column,
            tile_count,
            weight_in,
            bias_in.reshape(1, -1),
            weight_out,
            bias_out.reshape(1, -1),
        )

    placed = (
        P(("row", "col"), None),
        P(("row", "col"), None, None, None),
        P(("row", "col"), None),
        P(("row", "col"), None),
        P(("row", "col")),
        P(),
        P(),
        P(),
        P(),
    )
    return jax.shard_map(
        shards, mesh=mesh, in_specs=placed, out_specs=P(("row", "col"), None), check_vma=False
    )
```
